256 devices in a mesh: panel: 2 (over core), gx: 32 (over x, z), gy: 4 (over y).
Axes of the slice: x: 4, y: 4, z: 8, core: 2. Of those that a mesh axis runs over, the one named last changes fastest.
Arguments:
- model_state: float32 [2, 2048, 40, 512], P('panel', 'gx', None, 'gy'), may hold values from -6 to 6
- depart_frac: float32 [2, 2048, 512], P('panel', 'gx', 'gy'), may hold values from 0 to 1
- depart_cell: int32 [2, 2048, 512], P('panel', 'gx', 'gy'), may hold values from 1 to 125
- row_source: int32 [2, 8192], P('panel', ('gx', 'gy')), may hold values from 0 to 255, as said below
- send_block: int32 [2, 128, 128, 2], P('panel', ('gx', 'gy')), may hold values from -1 to 63, as said below
- strip_from: int32 [2, 128, 512], P('panel', ('gx', 'gy')), may hold values from 0 to 8191
- strip_into: int32 [2, 128, 512], P('panel', ('gx', 'gy')), may hold values from 0 to 8191, as said below
- helmholtz_coef: float32 [40], replicated, may hold values from 0.25 to 4
- vertical_mix: float32 [40, 40], replicated, may hold values from -1 to 1
Outputs:
- balanced: float32 [2, 2048, 40, 512], P('panel', 'gx', None, 'gy')
The draws below stay inside these ranges and needn't reach their ends.
Inputs may be any that keep to these rules, and one draw needn't show every extreme that they name: `row_source`: slot k (below 2) of source tile s is named s * 2 + k; the 64 rows of one tile name distinct slots, and every tile takes all 2 slots of itself. `send_block`: A block index, or -1 for an empty slot; exactly the slots named in row_source are filled. `strip_into`: the 512 cells of one tile are distinct.
All inputs are finite; a program needn't handle non-finite values.
Results may differ from the reference program's by a relative error of at most 0.000067.
Values sent between devices are 32-bit elements; how exact they have to be, the bound alone decides.
No kernel may reach another device: no remote copies, remote signals or barrier semaphores. Data moves between devices by JAX's collectives and lax.ppermute only.
A program may use at most 64 MiB of HBM per device.

```python
import math
import jax
import jax.numpy as jnp
from jax import lax

CX = 64
CY = 128
SWEEPS = 8
SW = 512
CHAN = 40
NG = 128
CAP = 2
NX = 2048
NY = 512
N_GX = 32
N_GY = 4


def routing(key):
    number_of_tiles = N_GX * N_GY
    total_slots = number_of_tiles * CAP
    key_reach = jax.random.fold_in(key, 101)
    key_ranking = jax.random.fold_in(key, 102)
    key_order = jax.random.fold_in(key, 103)
    key_block = jax.random.fold_in(key, 104)
    stencil_extent = jax.random.randint(key_reach, (2, number_of_tiles, 1), 1, N_GX + 1)
    target_panel = jnp.arange(number_of_tiles, dtype=jnp.int32)[None, :, None]
    slot_ids = jnp.arange(total_slots, dtype=jnp.int32)[None, None, :]
    sending_panel = slot_ids // CAP
    shift_amount = (target_panel // N_GY - sending_panel // N_GY) % N_GX
    extra_credit = jnp.where((sending_panel % N_GY == target_panel % N_GY) & (shift_amount < stencil_extent), 1, 0)
    local_owner = jnp.where(sending_panel == target_panel, 1, 0)
    ranking_value = jax.random.randint(key_ranking, (2, number_of_tiles, total_slots), 0, 65536) + extra_credit * 131072 + local_owner * 262144
    ranking_value = ranking_value * total_slots + slot_ids
    chosen = lax.top_k(ranking_value, CX)[1].astype(jnp.int32)
    row_key = jax.random.randint(key_order, (2, number_of_tiles, CX), 0, 65536) * CX + jnp.arange(CX, dtype=jnp.int32)
    order = jnp.argsort(row_key, axis=-1, stable=True)
    row_slots = jnp.take_along_axis(chosen, order, axis=-1)
    blocks = jax.random.randint(key_block, (2, number_of_tiles, CX), 0, CX)
    blocks = blocks.at[:, 0, 0].set(CX - 1)
    panel_ids = jnp.arange(2, dtype=jnp.int32)[:, None, None]
    sender_table = jnp.full((2, number_of_tiles, number_of_tiles, CAP), -1, jnp.int32)
    sender_table = sender_table.at[panel_ids, row_slots // CAP, target_panel, row_slots % CAP].set(blocks)
    return (row_slots.reshape(2, number_of_tiles * CX), sender_table)


def draw_row_source(key, part):
    return routing(key)[0]


def draw_send_block(key, part):
    return routing(key)[1]


def pick_cells(single):
    first_key = jax.random.fold_in(single, 1)
    second_key = jax.random.fold_in(single, 2)
    middle = jax.random.permutation(first_key, CX * CY - 2)[:SW - 2].astype(jnp.int32) + 1
    ends = jnp.array([0, CX * CY - 1], dtype=jnp.int32)
    joined = jnp.concatenate([ends, middle])
    return jax.random.permutation(second_key, joined)


def draw_strip_into(key, part):
    key = jax.random.fold_in(key, 7)
    keys = jax.random.split(key, 2 * N_GX * N_GY)
    picked = jax.vmap(pick_cells)(keys)
    return picked.astype(jnp.int32).reshape(2, N_GX * N_GY, SW)


def with_ends(values, own_key, low, top_value):
    extent = values.shape
    index_at = [jax.random.randint(jax.random.fold_in(own_key, axis), (), 0, extent[axis]) for axis in range(len(extent))]
    values = values.at[tuple(index_at)].set(low)
    longest = extent.index(max(extent))
    index_at[longest] = (index_at[longest] + 1) % extent[longest]
    return values.at[tuple(index_at)].set(top_value)


def steps_of(own_key, extent, cuts, least, largest):
    level = 1.0
    for axis_at, shards_of in cuts:
        steps = jax.random.uniform(jax.random.fold_in(jax.random.fold_in(own_key, 6), axis_at), (shards_of,), jnp.float32, least / len(cuts), largest / len(cuts))
        level = level * jnp.repeat(jnp.exp(steps), extent[axis_at] // shards_of).reshape((-1,) + (1,) * (len(extent) - 1 - axis_at))
    return level


def centred(rng, shape, width, bound, shards=(), kind=jnp.bfloat16):
    result = jax.random.normal(rng, shape, jnp.float32) * width
    if len(shards) > 0:
        result = steps_of(rng, shape, shards, -0.22, 0.18) * result
    return jnp.clip(result, min=-bound, max=bound).astype(kind)


def setup_inputs(seed: int = 0) -> dict:
    arg_keys = jax.random.split(jax.random.key(seed), 10)
    return {
        "model_state": centred(arg_keys[0], (2, NX, CHAN, NY), 1.0, 6.0, ((0, 2), (1, 32), (3, 4)), jnp.float32),
        "depart_frac": jnp.clip(1.0 * jax.random.uniform(arg_keys[1], (2, NX, NY), jnp.float32) ** steps_of(arg_keys[1], (2, NX, NY), ((0, 2), (1, 32), (2, 4)), -0.2, 0.2), 0.0, 1.0),
        "depart_cell": with_ends(jax.random.randint(arg_keys[2], (2, NX, NY), 1, CY - 2), jax.random.fold_in(arg_keys[2], 1), 1, (CY - 2) - 1).astype(jnp.int32),
        "row_source": draw_row_source(jax.random.fold_in(arg_keys[9], 71), 0),
        "send_block": draw_send_block(jax.random.fold_in(arg_keys[9], 71), 0),
        "strip_from": with_ends(jax.random.randint(arg_keys[5], (2, NG, SW), 0, CX * CY), jax.random.fold_in(arg_keys[5], 1), 0, (CX * CY) - 1).astype(jnp.int32),
        "strip_into": draw_strip_into(jax.random.fold_in(arg_keys[9], 71), 0),
        "helmholtz_coef": jnp.clip(jnp.exp(jax.random.uniform(arg_keys[7], (CHAN,), jnp.float32, math.log(0.25), math.log(4.0))), 0.25, 4.0),
        "vertical_mix": centred(arg_keys[8], (CHAN, CHAN), CHAN ** -0.5, 1.0, (), jnp.float32),
    }


def cubic_sample(block_rows, cell_index, fraction):
    weight_a = -fraction * (fraction - 1.0) * (fraction - 2.0) / 6.0
    weight_b = (fraction + 1.0) * (fraction - 1.0) * (fraction - 2.0) / 2.0
    weight_c = -(fraction + 1.0) * fraction * (fraction - 2.0) / 2.0
    weight_d = (fraction + 1.0) * fraction * (fraction - 1.0) / 6.0

    def tap(shift_amount):
        where_at = jnp.broadcast_to(jnp.expand_dims(cell_index + shift_amount, -2), block_rows.shape)
        return jnp.take_along_axis(block_rows, where_at, axis=-1)

    return (jnp.expand_dims(weight_a, -2) * tap(-1) + jnp.expand_dims(weight_b, -2) * tap(0)
            + jnp.expand_dims(weight_c, -2) * tap(1) + jnp.expand_dims(weight_d, -2) * tap(2))


def reference(model_state, depart_frac, depart_cell, row_source, send_block, strip_from, strip_into, helmholtz_coef, vertical_mix):
    number_of_tiles = N_GX * N_GY
    tiles = model_state.reshape(2, N_GX, CX, CHAN, N_GY, CY).transpose(0, 1, 4, 2, 3, 5).reshape(2, number_of_tiles, CX, CHAN, CY)
    frac_tiles = depart_frac.reshape(2, N_GX, CX, N_GY, CY).transpose(0, 1, 3, 2, 4).reshape(2, number_of_tiles, CX, CY)
    cell_tiles = depart_cell.reshape(2, N_GX, CX, N_GY, CY).transpose(0, 1, 3, 2, 4).reshape(2, number_of_tiles, CX, CY)
    slots = row_source.reshape(2, number_of_tiles, CX)
    source_dev = slots // CAP
    slot_no = slots % CAP
    panel_ids = jnp.arange(2, dtype=jnp.int32)[:, None, None]
    device_ids = jnp.arange(number_of_tiles, dtype=jnp.int32)[None, :, None]
    block_ids = send_block[panel_ids, source_dev, device_ids, slot_no]
    fetched = tiles[panel_ids, source_dev, block_ids]
    interp = cubic_sample(fetched, cell_tiles, frac_tiles)
    coupled = jnp.einsum("pdxgy,gf->pdxfy", tiles, vertical_mix, precision=lax.Precision.HIGHEST)
    arrival = interp + 0.5 * coupled
    strip_vals = arrival[panel_ids, device_ids, strip_from // CY, :, strip_from % CY]
    received = strip_vals[::-1]
    merged = arrival.at[panel_ids, device_ids, strip_into // CY, :, strip_into % CY].set(received)
    merged_grid = merged.reshape(2, N_GX, N_GY, CX, CHAN, CY).transpose(0, 1, 3, 4, 2, 5).reshape(2, NX, CHAN, NY)
    coeff = helmholtz_coef[None, None, :, None]
    diagonal = 1.0 + 4.0 * coeff
    balanced = merged_grid
    for sweep_no in range(SWEEPS):
        padded = jnp.pad(balanced, ((0, 0), (1, 1), (0, 0), (1, 1)))
        neighbours = padded[:, 2:, :, 1:-1] + padded[:, :-2, :, 1:-1] + padded[:, 1:-1, :, 2:] + padded[:, 1:-1, :, :-2]
        balanced = (merged_grid + coeff * neighbours) / diagonal
    return balanced
```

```python
import functools

import jax
import jax.numpy as jnp
from jax import lax
from jax.experimental import pallas as pl
from jax.experimental.pallas import tpu as pltpu
from jax.sharding import PartitionSpec as P

SWEEPS = 8
WIDTH = 8
SUB = 8
F32 = jnp.float32
VMEM_LIMIT = 48 * 1024 * 1024


def whole(space=pltpu.VMEM):
    return pl.BlockSpec(memory_space=space)


def params():
    return pltpu.CompilerParams(vmem_limit_bytes=VMEM_LIMIT)


def cost(flops, moved):
    return pl.CostEstimate(flops=flops, bytes_accessed=moved, transcendentals=0)


def pack_kernel(wanted, tile, out, sem):
    slots, tiles = wanted.shape

    def send(d, sent):
        for k in range(slots):
            block = wanted[k, d]
            filled = block >= 0

            @pl.when(filled)
            def _():
                pltpu.make_async_copy(tile.at[block], out.at[d, k], sem).start()

            sent = sent + jnp.where(filled, 1, 0)
        return sent

    sent = lax.fori_loop(0, tiles, send, 0)

    def wait(_, carry):
        pltpu.make_async_copy(tile.at[0], out.at[0, 0], sem).wait()
        return carry

    lax.fori_loop(0, sent, wait, 0)


def pack_blocks(wanted, tile):
    slots, tiles = wanted.shape
    return pl.pallas_call(
        pack_kernel,
        out_shape=jax.ShapeDtypeStruct((tiles, slots) + tile.shape[1:], F32),
        in_specs=[whole(pltpu.SMEM), whole()],
        out_specs=whole(pl.ANY),
        scratch_shapes=[pltpu.SemaphoreType.DMA],
        compiler_params=params(),
        name="pack_blocks",
    )(wanted, tile)


def couple_kernel(tile, mix_t, out):
    mix = mix_t[...] * 0.5

    def row(r, carry):
        out[r] = jnp.dot(mix, tile[r], precision=lax.Precision.HIGHEST, preferred_element_type=F32)
        return carry

    lax.fori_loop(0, tile.shape[0], row, 0, unroll=4)


def couple(tile, mix_t):
    return pl.pallas_call(
        couple_kernel,
        out_shape=jax.ShapeDtypeStruct(tile.shape, F32),
        in_specs=[whole(), whole()],
        out_specs=whole(),
        compiler_params=params(),
        cost_estimate=cost(2 * tile.size * tile.shape[1] * 6, 8 * tile.size),
        name="couple",
    )(tile, mix_t)


def arrive_kernel(rows, strip, slots, coupled, cell, frac, out, picked, fetched, sem):
    count, chan, cells = out.shape

    def fetch(r, carry):
        pltpu.make_async_copy(slots.at[rows[0, r]], fetched.at[r], sem).start()
        return carry

    lax.fori_loop(0, count, fetch, 0)
    pltpu.make_async_copy(slots.at[pl.ds(0, count)], fetched, sem).wait()

    def row(r, carry):
        t = frac[pl.ds(r, 1), :]
        m = jnp.broadcast_to(cell[pl.ds(r, 1), :], (SUB, cells))
        weights = (
            -t * (t - 1.0) * (t - 2.0) / 6.0,
            (t + 1.0) * (t - 1.0) * (t - 2.0) / 2.0,
            -(t + 1.0) * t * (t - 2.0) / 2.0,
            (t + 1.0) * t * (t - 1.0) / 6.0,
        )
        weights = [jnp.broadcast_to(w, (SUB, cells)) for w in weights]
        for c in range(0, chan, SUB):
            block = fetched[r, c : c + SUB, :]
            total = coupled[r, c : c + SUB, :]
            for tap, weight in zip((-1, 0, 1, 2), weights):
                total = total + weight * jnp.take_along_axis(
                    block, m + tap, axis=1, mode="promise_in_bounds"
                )
            out[r, c : c + SUB, :] = total
        return carry

    lax.fori_loop(0, count, row, 0, unroll=2)

    lane = lax.broadcasted_iota(jnp.int32, (chan, cells), 1)
    for part in range(picked.shape[1] // cells):

        def pick(j, held):
            place = strip[0, part * cells + j]
            moved = pltpu.roll(out[place // cells], (j - place % cells) & (cells - 1), 1)
            return jnp.where(lane == j, moved, held)

        held = lax.fori_loop(0, cells, pick, jnp.zeros((chan, cells), F32), unroll=8)
        picked[:, part * cells : (part + 1) * cells] = held


def arrive(rows, strip, slots, coupled, cell, frac):
    return pl.pallas_call(
        arrive_kernel,
        out_shape=(
            jax.ShapeDtypeStruct(coupled.shape, F32),
            jax.ShapeDtypeStruct((coupled.shape[1], strip.shape[1]), F32),
        ),
        in_specs=[whole(pltpu.SMEM), whole(pltpu.SMEM), whole(pl.ANY), whole(), whole(), whole()],
        out_specs=(whole(), whole()),
        scratch_shapes=[pltpu.VMEM(coupled.shape, F32), pltpu.SemaphoreType.DMA],
        compiler_params=params(),
        name="arrive",
    )(rows, strip, slots, coupled, cell, frac)


def merge_kernel(strip, arrival, received, out, low, high):
    count, chan, cells = out.shape
    out[...] = arrival[...]
    lane = lax.broadcasted_iota(jnp.int32, (chan, cells), 1)
    for part in range(received.shape[1] // cells):

        def put(j, carry):
            place = strip[0, part * cells + j]
            at = place % cells
            moved = pltpu.roll(
                received[:, part * cells : (part + 1) * cells], (at - j) & (cells - 1), 1
            )
            pltpu.store(out.at[place // cells], moved, mask=lane == at)
            return carry

        lax.fori_loop(0, cells, put, 0, unroll=8)
    per = cells // WIDTH
    for g in range(count // per):

        def edge(i, held):
            row = out[g * per + i]
            here = (lane // WIDTH) == i
            first = pltpu.roll(row, i * WIDTH, 1)
            last = pltpu.roll(row, (i + 1) * WIDTH & (cells - 1), 1)
            return jnp.where(here, first, held[0]), jnp.where(here, last, held[1])

        empty = jnp.zeros((chan, cells), F32)
        low[g], high[g] = lax.fori_loop(0, per, edge, (empty, empty), unroll=4)


def merge(strip, arrival, received):
    count, chan, cells = arrival.shape
    edge = jax.ShapeDtypeStruct((count * WIDTH // cells, chan, cells), F32)
    return pl.pallas_call(
        merge_kernel,
        out_shape=(jax.ShapeDtypeStruct(arrival.shape, F32), edge, edge),
        in_specs=[whole(pltpu.SMEM), whole(), whole()],
        out_specs=(whole(), whole(), whole()),
        compiler_params=params(),
        name="merge",
    )(strip, arrival, received)


def edge_rows_kernel(merged, left, right, first, last):
    count, chan, cells = merged.shape
    lane = lax.broadcasted_iota(jnp.int32, (chan, cells), 1)
    half = cells // 2
    groups = left.shape[0]
    first[:WIDTH] = merged[:WIDTH]
    first[WIDTH] = jnp.where(lane < half, right[0], pltpu.roll(left[0], half, 1))
    last[:WIDTH] = merged[count - WIDTH :]
    last[WIDTH] = jnp.where(lane < half, pltpu.roll(right[groups - 1], half, 1), left[groups - 1])


def edge_rows(merged, left, right):
    count, chan, cells = merged.shape
    rows = jax.ShapeDtypeStruct((WIDTH + 1, chan, cells), F32)
    return pl.pallas_call(
        edge_rows_kernel,
        out_shape=(rows, rows),
        in_specs=[whole(), whole(), whole()],
        out_specs=(whole(), whole()),
        compiler_params=params(),
        name="edge_rows",
    )(merged, left, right)


def relax_kernel(inside, merged, above, below, left, right, coef, out, m0, m1, a0, a1, b0, b1):
    count, chan, cells = merged.shape
    lane = lax.broadcasted_iota(jnp.int32, (chan, cells), 1)
    is_right, is_left = lane < WIDTH, lane >= cells - WIDTH
    h = coef[...]
    inv = 1.0 / (1.0 + 4.0 * h)
    inv_b = jnp.broadcast_to(inv, (chan, cells))
    total = count + 2 * WIDTH
    per = cells // WIDTH
    half = cells // 2

    def load(at, row, beside):
        a0[at] = row
        m0[at] = row * inv_b
        a1[at] = beside
        m1[at] = beside * inv_b

    for at, rows in ((0, above), (WIDTH + count, below)):
        for i in range(WIDTH):
            packed = rows[WIDTH]
            beside = jnp.where(
                is_right,
                pltpu.roll(packed, (-i * WIDTH) % cells, 1),
                jnp.where(is_left, pltpu.roll(packed, (half - (i + 1) * WIDTH) % cells, 1), 0.0),
            )
            load(at + i, rows[i], beside)
    for g in range(left.shape[0]):

        def fill(i, carry):
            to_right = pltpu.roll(right[g], (cells - i * WIDTH) & (cells - 1), 1)
            to_left = pltpu.roll(left[g], cells - (i + 1) * WIDTH, 1)
            beside = jnp.where(is_right, to_right, jnp.where(is_left, to_left, 0.0))
            r = g * per + i
            load(WIDTH + r, merged[r], beside)
            return carry

        lax.fori_loop(0, per, fill, 0, unroll=4)

    lane8 = lax.broadcasted_iota(jnp.int32, (SUB, cells), 1)
    is_first, is_last = lane8 == 0, lane8 == cells - 1
    side = jnp.where(
        lane8 < WIDTH, inside[3], jnp.where(lane8 >= cells - WIDTH, inside[2], 0)
    ).astype(F32)

    def turn(row, beside):
        l0, l1 = pltpu.roll(row, 1, 1), pltpu.roll(beside, 1, 1)
        r0, r1 = pltpu.roll(row, cells - 1, 1), pltpu.roll(beside, cells - 1, 1)
        return (
            jnp.where(is_first, l1, l0) + jnp.where(is_last, r1, r0),
            jnp.where(is_first, l0, l1) + jnp.where(is_last, r0, r1),
        )

    for c in range(0, chan, SUB):
        ch = slice(c, c + SUB)
        gain = jnp.broadcast_to(h[ch] * inv[ch], (SUB, cells))
        gain_side = gain * side
        lo = inside[0].astype(F32)
        hi = inside[1].astype(F32)

        for s in range(SWEEPS):
            src0, src1 = (a0, a1) if s % 2 == 0 else (b0, b1)
            dst0, dst1 = (b0, b1) if s % 2 == 0 else (a0, a1)
            last = s == SWEEPS - 1
            begin, end = s + 1, total - s - 1

            def update(x, held, g0, g1):
                up0, up1, mid0, mid1 = held
                down0, down1 = src0[x + 1, ch], src1[x + 1, ch]
                across0, across1 = turn(mid0, mid1)
                new0 = m0[x, ch] + g0 * (up0 + down0 + across0)
                if last:
                    out[x - WIDTH, ch] = new0
                else:
                    dst0[x, ch] = new0
                    dst1[x, ch] = m1[x, ch] + g1 * (up1 + down1 + across1)
                return mid0, mid1, down0, down1

            held = (
                src0[begin - 1, ch],
                src1[begin - 1, ch],
                src0[begin, ch],
                src1[begin, ch],
            )
            for x in range(begin, WIDTH):
                held = update(x, held, gain * lo, gain_side * lo)
            held = lax.fori_loop(
                WIDTH,
                WIDTH + count,
                lambda x, v: update(x, v, gain, gain_side),
                held,
                unroll=8,
            )
            for x in range(WIDTH + count, end):
                held = update(x, held, gain * hi, gain_side * hi)


def relax(inside, merged, above, below, left, right, coef):
    count, chan, cells = merged.shape
    held = pltpu.VMEM((count + 2 * WIDTH, chan, cells), F32)
    return pl.pallas_call(
        relax_kernel,
        out_shape=jax.ShapeDtypeStruct(merged.shape, F32),
        in_specs=[whole(pltpu.SMEM)] + [whole()] * 6,
        out_specs=whole(),
        scratch_shapes=[held] * 6,
        compiler_params=params(),
        name="relax",
    )(inside, merged, above, below, left, right, coef)


def shifted(block, axis, step):
    count = lax.axis_size(axis)
    route = [(i, i + step) for i in range(count) if 0 <= i + step < count]
    return lax.ppermute(block, axis, route)


def local(
    model_state,
    depart_frac,
    depart_cell,
    row_source,
    send_block,
    strip_from,
    strip_into,
    helmholtz_coef,
    vertical_mix,
):
    tile = model_state[0]
    chan = tile.shape[1]
    outgoing = pack_blocks(send_block[0, 0].T, tile)
    arrived = lax.all_to_all(outgoing, ("gx", "gy"), split_axis=0, concat_axis=0, tiled=True)
    coupled = couple(tile, vertical_mix.T)
    slots = arrived.reshape((-1,) + tile.shape[1:])
    arrival, picked = arrive(
        row_source, strip_from[0], slots, coupled, depart_cell[0], depart_frac[0]
    )
    received = lax.ppermute(picked, "panel", [(0, 1), (1, 0)])
    merged, low, high = merge(strip_into[0], arrival, received)
    right = shifted(low, "gy", -1)
    left = shifted(high, "gy", 1)
    first, last = edge_rows(merged, left, right)
    below = shifted(first, "gx", -1)
    above = shifted(last, "gx", 1)
    gx, gy = lax.axis_index("gx"), lax.axis_index("gy")
    inside = jnp.stack(
        [gx > 0, gx < lax.axis_size("gx") - 1, gy > 0, gy < lax.axis_size("gy") - 1]
    ).astype(jnp.int32)
    balanced = relax(
        inside, merged, above, below, left, right, helmholtz_coef.reshape(chan, 1)
    )
    return balanced[None]


def solution(mesh):
    in_specs = (
        P("panel", "gx", None, "gy"),
        P("panel", "gx", "gy"),
        P("panel", "gx", "gy"),
        P("panel", ("gx", "gy")),
        P("panel", ("gx", "gy"), None, None),
        P("panel", ("gx", "gy"), None),
        P("panel", ("gx", "gy"), None),
        P(),
        P(),
    )
    out_specs = P("panel", "gx", None, "gy")
    return jax.shard_map(local, mesh=mesh, in_specs=in_specs, out_specs=out_specs, check_vma=False)
```

```python
import functools

import jax
import jax.numpy as jnp
from jax import lax
from jax.experimental import pallas as pl
from jax.experimental.pallas import tpu as pltpu
from jax.sharding import PartitionSpec as P

SWEEPS = 8
WIDTH = 8
SUB = 8
F32 = jnp.float32
VMEM_LIMIT = 48 * 1024 * 1024


def whole(space=pltpu.VMEM):
    return pl.BlockSpec(memory_space=space)


def params():
    return pltpu.CompilerParams(vmem_limit_bytes=VMEM_LIMIT)


def cost(flops, moved):
    return pl.CostEstimate(flops=flops, bytes_accessed=moved, transcendentals=0)


def pack_kernel(wanted, tile, out, sem):
    slots, tiles = wanted.shape

    def send(d, sent):
        for k in range(slots):
            block = wanted[k, d]
            filled = block >= 0

            @pl.when(filled)
            def _():
                pltpu.make_async_copy(tile.at[block], out.at[d, k], sem).start()

            sent = sent + jnp.where(filled, 1, 0)
        return sent

    sent = lax.fori_loop(0, tiles, send, 0)

    def wait(_, carry):
        pltpu.make_async_copy(tile.at[0], out.at[0, 0], sem).wait()
        return carry

    lax.fori_loop(0, sent, wait, 0)


def pack_blocks(wanted, tile):
    slots, tiles = wanted.shape
    return pl.pallas_call(
        pack_kernel,
        out_shape=jax.ShapeDtypeStruct((tiles, slots) + tile.shape[1:], F32),
        in_specs=[whole(pltpu.SMEM), whole()],
        out_specs=whole(pl.ANY),
        scratch_shapes=[pltpu.SemaphoreType.DMA],
        compiler_params=params(),
        name="pack_blocks",
    )(wanted, tile)


def couple_kernel(tile, mix_t, out):
    mix = mix_t[...] * 0.5

    def row(r, carry):
        out[r] = jnp.dot(mix, tile[r], precision=lax.Precision.HIGHEST, preferred_element_type=F32)
        return carry

    lax.fori_loop(0, tile.shape[0], row, 0, unroll=4)


def couple(tile, mix_t):
    return pl.pallas_call(
        couple_kernel,
        out_shape=jax.ShapeDtypeStruct(tile.shape, F32),
        in_specs=[whole(), whole()],
        out_specs=whole(),
        compiler_params=params(),
        cost_estimate=cost(2 * tile.size * tile.shape[1] * 6, 8 * tile.size),
        name="couple",
    )(tile, mix_t)


def arrive_kernel(rows, strip, slots, coupled, cell, frac, out, picked, fetched, sem):
    count, chan, cells = out.shape

    def fetch(r, carry):
        pltpu.make_async_copy(slots.at[rows[0, r]], fetched.at[r], sem).start()
        return carry

    lax.fori_loop(0, count, fetch, 0)
    pltpu.make_async_copy(slots.at[pl.ds(0, count)], fetched, sem).wait()

    def row(r, carry):
        t = frac[pl.ds(r, 1), :]
        m = jnp.broadcast_to(cell[pl.ds(r, 1), :], (SUB, cells))
        weights = (
            -t * (t - 1.0) * (t - 2.0) / 6.0,
            (t + 1.0) * (t - 1.0) * (t - 2.0) / 2.0,
            -(t + 1.0) * t * (t - 2.0) / 2.0,
            (t + 1.0) * t * (t - 1.0) / 6.0,
        )
        weights = [jnp.broadcast_to(w, (SUB, cells)) for w in weights]
        for c in range(0, chan, SUB):
            block = fetched[r, c : c + SUB, :]
            total = coupled[r, c : c + SUB, :]
            for tap, weight in zip((-1, 0, 1, 2), weights):
                total = total + weight * jnp.take_along_axis(
                    block, m + tap, axis=1, mode="promise_in_bounds"
                )
            out[r, c : c + SUB, :] = total
        return carry

    lax.fori_loop(0, count, row, 0, unroll=16)

    lane = lax.broadcasted_iota(jnp.int32, (chan, cells), 1)
    for part in range(picked.shape[1] // cells):

        def pick(j, held):
            place = strip[0, part * cells + j]
            moved = pltpu.roll(out[place // cells], (j - place % cells) & (cells - 1), 1)
            return jnp.where(lane == j, moved, held)

        held = lax.fori_loop(0, cells, pick, jnp.zeros((chan, cells), F32), unroll=True)
        picked[:, part * cells : (part + 1) * cells] = held


def arrive(rows, strip, slots, coupled, cell, frac):
    return pl.pallas_call(
        arrive_kernel,
        out_shape=(
            jax.ShapeDtypeStruct(coupled.shape, F32),
            jax.ShapeDtypeStruct((coupled.shape[1], strip.shape[1]), F32),
        ),
        in_specs=[whole(pltpu.SMEM), whole(pltpu.SMEM), whole(pl.ANY), whole(), whole(), whole()],
        out_specs=(whole(), whole()),
        scratch_shapes=[pltpu.VMEM(coupled.shape, F32), pltpu.SemaphoreType.DMA],
        compiler_params=params(),
        name="arrive",
    )(rows, strip, slots, coupled, cell, frac)


def merge_kernel(strip, arrival, received, out, low, high):
    count, chan, cells = out.shape
    out[...] = arrival[...]
    lane = lax.broadcasted_iota(jnp.int32, (chan, cells), 1)
    for part in range(received.shape[1] // cells):

        def put(j, carry):
            place = strip[0, part * cells + j]
            at = place % cells
            moved = pltpu.roll(
                received[:, part * cells : (part + 1) * cells], (at - j) & (cells - 1), 1
            )
            pltpu.store(out.at[place // cells], moved, mask=lane == at)
            return carry

        lax.fori_loop(0, cells, put, 0, unroll=32)
    per = cells // WIDTH
    for g in range(count // per):

        def edge(i, held):
            row = out[g * per + i]
            here = (lane // WIDTH) == i
            first = pltpu.roll(row, i * WIDTH, 1)
            last = pltpu.roll(row, (i + 1) * WIDTH & (cells - 1), 1)
            return jnp.where(here, first, held[0]), jnp.where(here, last, held[1])

        empty = jnp.zeros((chan, cells), F32)
        low[g], high[g] = lax.fori_loop(0, per, edge, (empty, empty), unroll=True)


def merge(strip, arrival, received):
    count, chan, cells = arrival.shape
    edge = jax.ShapeDtypeStruct((count * WIDTH // cells, chan, cells), F32)
    return pl.pallas_call(
        merge_kernel,
        out_shape=(jax.ShapeDtypeStruct(arrival.shape, F32), edge, edge),
        in_specs=[whole(pltpu.SMEM), whole(), whole()],
        out_specs=(whole(), whole(), whole()),
        compiler_params=params(),
        name="merge",
    )(strip, arrival, received)


def edge_rows_kernel(merged, left, right, first, last):
    count, chan, cells = merged.shape
    lane = lax.broadcasted_iota(jnp.int32, (chan, cells), 1)
    half = cells // 2
    groups = left.shape[0]
    first[:WIDTH] = merged[:WIDTH]
    first[WIDTH] = jnp.where(lane < half, right[0], pltpu.roll(left[0], half, 1))
    last[:WIDTH] = merged[count - WIDTH :]
    last[WIDTH] = jnp.where(lane < half, pltpu.roll(right[groups - 1], half, 1), left[groups - 1])


def edge_rows(merged, left, right):
    count, chan, cells = merged.shape
    rows = jax.ShapeDtypeStruct((WIDTH + 1, chan, cells), F32)
    return pl.pallas_call(
        edge_rows_kernel,
        out_shape=(rows, rows),
        in_specs=[whole(), whole(), whole()],
        out_specs=(whole(), whole()),
        compiler_params=params(),
        name="edge_rows",
    )(merged, left, right)


def relax_kernel(inside, merged, above, below, left, right, coef, out, a0, a1, b0, b1, start1):
    count, chan, cells = merged.shape
    lane = lax.broadcasted_iota(jnp.int32, (chan, cells), 1)
    is_right, is_left = lane < WIDTH, lane >= cells - WIDTH
    h = coef[...]
    inv = 1.0 / (1.0 + 4.0 * h)
    total = count + 2 * WIDTH
    per = cells // WIDTH
    half = cells // 2

    for at, rows in ((0, above), (WIDTH + count, below)):
        for i in range(WIDTH):
            packed = rows[WIDTH]
            start1[at + i] = jnp.where(
                is_right,
                pltpu.roll(packed, (-i * WIDTH) % cells, 1),
                jnp.where(is_left, pltpu.roll(packed, (half - (i + 1) * WIDTH) % cells, 1), 0.0),
            )
    for r in range(count):
        g, i = divmod(r, per)
        start1[WIDTH + r] = jnp.where(
            is_right,
            pltpu.roll(right[g], (-i * WIDTH) % cells, 1),
            jnp.where(is_left, pltpu.roll(left[g], (-(i + 1) * WIDTH) % cells, 1), 0.0),
        )

    lane8 = lax.broadcasted_iota(jnp.int32, (SUB, cells), 1)
    is_first, is_last = lane8 == 0, lane8 == cells - 1
    side = jnp.where(
        lane8 < WIDTH, inside[3], jnp.where(lane8 >= cells - WIDTH, inside[2], 0)
    ).astype(F32)
    lo, hi = inside[0].astype(F32), inside[1].astype(F32)

    def turn(row, beside):
        l0, l1 = pltpu.roll(row, 1, 1), pltpu.roll(beside, 1, 1)
        r0, r1 = pltpu.roll(row, cells - 1, 1), pltpu.roll(beside, cells - 1, 1)
        return (
            jnp.where(is_first, l1, l0) + jnp.where(is_last, r1, r0),
            jnp.where(is_first, l0, l1) + jnp.where(is_last, r0, r1),
        )

    def first_row(x, ch):
        if x < WIDTH:
            return above[x, ch]
        return merged[x - WIDTH, ch] if x < WIDTH + count else below[x - WIDTH - count, ch]

    for c in range(0, chan, SUB):
        ch = slice(c, c + SUB)
        inv8 = jnp.broadcast_to(inv[ch], (SUB, cells))
        gain = jnp.broadcast_to(h[ch] * inv[ch], (SUB, cells))
        gain_side = gain * side

        for s in range(SWEEPS):
            now, later = ((a0, a1), (b0, b1))[:: 1 if s % 2 else -1]
            begin, end = s + 1, total - s - 1

            def held(x):
                if s == 0:
                    return first_row(x, ch), start1[x, ch]
                return now[0][x, ch], now[1][x, ch]

            up, mid = held(begin - 1), held(begin)
            for x in range(begin, end):
                down = held(x + 1)
                across = turn(*mid)
                part = lo if x < WIDTH else hi if x >= WIDTH + count else None
                g0 = gain if part is None else gain * part
                new = first_row(x, ch) * inv8 + g0 * (up[0] + down[0] + across[0])
                if s == SWEEPS - 1:
                    out[x - WIDTH, ch] = new
                else:
                    later[0][x, ch] = new
                    g1 = gain_side if part is None else gain_side * part
                    later[1][x, ch] = start1[x, ch] * inv8 + g1 * (up[1] + down[1] + across[1])
                up, mid = mid, down


def relax(inside, merged, above, below, left, right, coef):
    count, chan, cells = merged.shape
    held = pltpu.VMEM((count + 2 * WIDTH, chan, cells), F32)
    return pl.pallas_call(
        relax_kernel,
        out_shape=jax.ShapeDtypeStruct(merged.shape, F32),
        in_specs=[whole(pltpu.SMEM)] + [whole()] * 6,
        out_specs=whole(),
        scratch_shapes=[held] * 5,
        compiler_params=params(),
        name="relax",
    )(inside, merged, above, below, left, right, coef)


def shifted(block, axis, step):
    count = lax.axis_size(axis)
    route = [(i, i + step) for i in range(count) if 0 <= i + step < count]
    return lax.ppermute(block, axis, route)


def local(
    model_state,
    depart_frac,
    depart_cell,
    row_source,
    send_block,
    strip_from,
    strip_into,
    helmholtz_coef,
    vertical_mix,
):
    tile = model_state[0]
    chan = tile.shape[1]
    outgoing = pack_blocks(send_block[0, 0].T, tile)
    arrived = lax.all_to_all(outgoing, ("gx", "gy"), split_axis=0, concat_axis=0, tiled=True)
    coupled = couple(tile, vertical_mix.T)
    slots = arrived.reshape((-1,) + tile.shape[1:])
    arrival, picked = arrive(
        row_source, strip_from[0], slots, coupled, depart_cell[0], depart_frac[0]
    )
    received = lax.ppermute(picked, "panel", [(0, 1), (1, 0)])
    merged, low, high = merge(strip_into[0], arrival, received)
    right = shifted(low, "gy", -1)
    left = shifted(high, "gy", 1)
    first, last = edge_rows(merged, left, right)
    below = shifted(first, "gx", -1)
    above = shifted(last, "gx", 1)
    gx, gy = lax.axis_index("gx"), lax.axis_index("gy")
    inside = jnp.stack(
        [gx > 0, gx < lax.axis_size("gx") - 1, gy > 0, gy < lax.axis_size("gy") - 1]
    ).astype(jnp.int32)
    balanced = relax(
        inside, merged, above, below, left, right, helmholtz_coef.reshape(chan, 1)
    )
    return balanced[None]


def solution(mesh):
    in_specs = (
        P("panel", "gx", None, "gy"),
        P("panel", "gx", "gy"),
        P("panel", "gx", "gy"),
        P("panel", ("gx", "gy")),
        P("panel", ("gx", "gy"), None, None),
        P("panel", ("gx", "gy"), None),
        P("panel", ("gx", "gy"), None),
        P(),
        P(),
    )
    out_specs = P("panel", "gx", None, "gy")
    return jax.shard_map(local, mesh=mesh, in_specs=in_specs, out_specs=out_specs, check_vma=False)
```

```python
import functools

import jax
import jax.numpy as jnp
from jax import lax
from jax.experimental import pallas as pl
from jax.experimental.pallas import tpu as pltpu
from jax.sharding import PartitionSpec as P

SWEEPS = 8
WIDTH = 8
PARTS = 4
SUB = 8
F32 = jnp.float32
VMEM_LIMIT = 48 * 1024 * 1024
PACK_LIMIT = 63 * 1024 * 1024


def whole(space=pltpu.VMEM):
    return pl.BlockSpec(memory_space=space)


def params():
    return pltpu.CompilerParams(vmem_limit_bytes=VMEM_LIMIT)


def cost(flops, moved):
    return pl.CostEstimate(flops=flops, bytes_accessed=moved, transcendentals=0)


def split(place, cells):
    return lax.shift_right_logical(place, cells.bit_length() - 1), place & (cells - 1)


def pack_kernel(listed, tile, out, wanted, sem):
    slots, tiles = wanted.shape
    pltpu.sync_copy(listed, wanted)

    def send(d, sent):
        for k in range(slots):
            block = wanted[k, d]
            filled = block >= 0

            @pl.when(filled)
            def _():
                pltpu.make_async_copy(tile.at[block], out.at[d, k], sem).start()

            sent = sent + jnp.where(filled, 1, 0)
        return sent

    sent = lax.fori_loop(0, tiles, send, 0, unroll=4)

    def wait(_, carry):
        pltpu.make_async_copy(tile.at[0], out.at[0, 0], sem).wait()
        return carry

    lax.fori_loop(0, sent, wait, 0)


def pack_blocks(wanted, tile):
    slots, tiles = wanted.shape
    return pl.pallas_call(
        pack_kernel,
        out_shape=jax.ShapeDtypeStruct((tiles, slots) + tile.shape[1:], F32),
        in_specs=[whole(pltpu.HBM), whole(pltpu.HBM)],
        out_specs=whole(pl.ANY),
        scratch_shapes=[pltpu.SMEM(wanted.shape, jnp.int32), pltpu.SemaphoreType.DMA],
        compiler_params=pltpu.CompilerParams(vmem_limit_bytes=PACK_LIMIT),
        name="pack_blocks",
    )(wanted, tile)


def couple_kernel(tile, mix_t, out):
    mix = mix_t[...] * 0.5

    def row(r, carry):
        out[r] = jnp.dot(mix, tile[r], precision=lax.Precision.HIGHEST, preferred_element_type=F32)
        return carry

    lax.fori_loop(0, tile.shape[0], row, 0, unroll=4)


def couple(tile, mix_t):
    return pl.pallas_call(
        couple_kernel,
        out_shape=jax.ShapeDtypeStruct(tile.shape, F32),
        in_specs=[whole(), whole()],
        out_specs=whole(),
        compiler_params=params(),
        cost_estimate=cost(2 * tile.size * tile.shape[1] * 6, 8 * tile.size),
        name="couple",
    )(tile, mix_t)


def arrive_kernel(rows, strip, slots, coupled, cell, frac, out, picked, fetched, sem):
    count, chan, cells = out.shape

    step = count // PARTS

    def fetch(r, carry, part):
        pltpu.make_async_copy(slots.at[rows[0, r]], fetched.at[r], sem.at[part]).start()
        return carry

    for part in range(PARTS):
        lax.fori_loop(
            part * step, (part + 1) * step, functools.partial(fetch, part=part), 0, unroll=True
        )

    def row(r, carry):
        t = frac[pl.ds(r, 1), :]
        m = jnp.broadcast_to(cell[pl.ds(r, 1), :], (SUB, cells))
        weights = (
            -t * (t - 1.0) * (t - 2.0) / 6.0,
            (t + 1.0) * (t - 1.0) * (t - 2.0) / 2.0,
            -(t + 1.0) * t * (t - 2.0) / 2.0,
            (t + 1.0) * t * (t - 1.0) / 6.0,
        )
        weights = [jnp.broadcast_to(w, (SUB, cells)) for w in weights]
        for c in range(0, chan, SUB):
            block = fetched[r, c : c + SUB, :]
            total = coupled[r, c : c + SUB, :]
            for tap, weight in zip((-1, 0, 1, 2), weights):
                total = total + weight * jnp.take_along_axis(
                    block, m + tap, axis=1, mode="promise_in_bounds"
                )
            out[r, c : c + SUB, :] = total
        return carry

    for part in range(PARTS):
        here = pl.ds(part * step, step)
        pltpu.make_async_copy(slots.at[here], fetched.at[here], sem.at[part]).wait()
        lax.fori_loop(part * step, (part + 1) * step, row, 0, unroll=True)

    lane = lax.broadcasted_iota(jnp.int32, (chan, cells), 1)
    for part in range(picked.shape[1] // cells):

        def pick(j, held):
            place = strip[0, part * cells + j]
            row, at = split(place, cells)
            moved = pltpu.roll(out[row], (j - at) & (cells - 1), 1)
            return jnp.where(lane == j, moved, held)

        held = lax.fori_loop(0, cells, pick, jnp.zeros((chan, cells), F32), unroll=True)
        picked[:, part * cells : (part + 1) * cells] = held


def arrive(rows, strip, slots, coupled, cell, frac):
    return pl.pallas_call(
        arrive_kernel,
        out_shape=(
            jax.ShapeDtypeStruct(coupled.shape, F32),
            jax.ShapeDtypeStruct((coupled.shape[1], strip.shape[1]), F32),
        ),
        in_specs=[whole(pltpu.SMEM), whole(pltpu.SMEM), whole(pl.ANY), whole(), whole(), whole()],
        out_specs=(whole(), whole()),
        scratch_shapes=[pltpu.VMEM(coupled.shape, F32), pltpu.SemaphoreType.DMA((PARTS,))],
        compiler_params=params(),
        name="arrive",
    )(rows, strip, slots, coupled, cell, frac)


def merge_kernel(strip, arrival, received, out, low, high, first, last):
    count, chan, cells = out.shape
    out[...] = arrival[...]
    lane = lax.broadcasted_iota(jnp.int32, (chan, cells), 1)
    for part in range(received.shape[1] // cells):

        def put(j, carry):
            place = strip[0, part * cells + j]
            row, at = split(place, cells)
            moved = pltpu.roll(
                received[:, part * cells : (part + 1) * cells], (at - j) & (cells - 1), 1
            )
            pltpu.store(out.at[row], moved, mask=lane == at)
            return carry

        lax.fori_loop(0, cells, put, 0, unroll=32)
    first[...] = out[:WIDTH]
    last[...] = out[count - WIDTH :]
    per = cells // WIDTH
    for g in range(count // per):

        def edge(i, held):
            row = out[g * per + i]
            here = (lane // WIDTH) == i
            left = pltpu.roll(row, i * WIDTH, 1)
            right = pltpu.roll(row, (i + 1) * WIDTH & (cells - 1), 1)
            return jnp.where(here, left, held[0]), jnp.where(here, right, held[1])

        empty = jnp.zeros((chan, cells), F32)
        low[g], high[g] = lax.fori_loop(0, per, edge, (empty, empty), unroll=True)


def merge(strip, arrival, received):
    count, chan, cells = arrival.shape
    edge = jax.ShapeDtypeStruct((count * WIDTH // cells, chan, cells), F32)
    rows = jax.ShapeDtypeStruct((WIDTH, chan, cells), F32)
    return pl.pallas_call(
        merge_kernel,
        out_shape=(jax.ShapeDtypeStruct(arrival.shape, F32), edge, edge, rows, rows),
        in_specs=[whole(pltpu.SMEM), whole(), whole()],
        out_specs=(whole(),) * 5,
        compiler_params=params(),
        name="merge",
    )(strip, arrival, received)


def corners_kernel(left, right, first, last):
    groups, chan, cells = left.shape
    lane = lax.broadcasted_iota(jnp.int32, (chan, cells), 1)
    half = cells // 2
    first[...] = jnp.where(lane < half, right[0], pltpu.roll(left[0], half, 1))
    last[...] = jnp.where(lane < half, pltpu.roll(right[groups - 1], half, 1), left[groups - 1])


def corners(left, right):
    held = jax.ShapeDtypeStruct(left.shape[1:], F32)
    return pl.pallas_call(
        corners_kernel,
        out_shape=(held, held),
        in_specs=[whole(), whole()],
        out_specs=(whole(), whole()),
        compiler_params=params(),
        name="corners",
    )(left, right)


def relax_kernel(
    inside,
    merged,
    above,
    below,
    above_side,
    below_side,
    left,
    right,
    coef,
    result,
    out,
    a0,
    a1,
    b0,
    b1,
    start1,
    sem,
):
    count, chan, cells = merged.shape
    lane = lax.broadcasted_iota(jnp.int32, (chan, cells), 1)
    is_right, is_left = lane < WIDTH, lane >= cells - WIDTH
    h = coef[...]
    inv = 1.0 / (1.0 + 4.0 * h)
    total = count + 2 * WIDTH
    per = cells // WIDTH
    half = cells // 2

    for at, rows in ((0, above_side), (WIDTH + count, below_side)):
        packed = rows[...]
        for i in range(WIDTH):
            start1[at + i] = jnp.where(
                is_right,
                pltpu.roll(packed, (-i * WIDTH) % cells, 1),
                jnp.where(is_left, pltpu.roll(packed, (half - (i + 1) * WIDTH) % cells, 1), 0.0),
            )
    for r in range(count):
        g, i = divmod(r, per)
        start1[WIDTH + r] = jnp.where(
            is_right,
            pltpu.roll(right[g], (-i * WIDTH) % cells, 1),
            jnp.where(is_left, pltpu.roll(left[g], (-(i + 1) * WIDTH) % cells, 1), 0.0),
        )

    lane8 = lax.broadcasted_iota(jnp.int32, (SUB, cells), 1)
    is_first, is_last = lane8 == 0, lane8 == cells - 1
    side = jnp.where(
        lane8 < WIDTH, inside[3], jnp.where(lane8 >= cells - WIDTH, inside[2], 0)
    ).astype(F32)
    lo, hi = inside[0].astype(F32), inside[1].astype(F32)

    def turn(row, beside):
        l0, l1 = pltpu.roll(row, 1, 1), pltpu.roll(beside, 1, 1)
        r0, r1 = pltpu.roll(row, cells - 1, 1), pltpu.roll(beside, cells - 1, 1)
        return (
            jnp.where(is_first, l1, l0) + jnp.where(is_last, r1, r0),
            jnp.where(is_first, l0, l1) + jnp.where(is_last, r0, r1),
        )

    def first_row(x, ch):
        if x < WIDTH:
            return above[x, ch]
        return merged[x - WIDTH, ch] if x < WIDTH + count else below[x - WIDTH - count, ch]

    for c in range(0, chan, SUB):
        ch = slice(c, c + SUB)
        inv8 = jnp.broadcast_to(inv[ch], (SUB, cells))
        gain = jnp.broadcast_to(h[ch] * inv[ch], (SUB, cells))
        gain_side = gain * side

        for s in range(SWEEPS):
            now, later = ((a0, a1), (b0, b1))[:: 1 if s % 2 else -1]
            begin, end = s + 1, total - s - 1

            def held(x):
                if s == 0:
                    return first_row(x, ch), start1[x, ch]
                return now[0][x, ch], now[1][x, ch]

            up, mid = held(begin - 1), held(begin)
            for x in range(begin, end):
                down = held(x + 1)
                across = turn(*mid)
                part = lo if x < WIDTH else hi if x >= WIDTH + count else None
                g0 = gain if part is None else gain * part
                new = first_row(x, ch) * inv8 + g0 * (up[0] + down[0] + across[0])
                if s == SWEEPS - 1:
                    out[x - WIDTH, ch] = new
                else:
                    later[0][x, ch] = new
                    g1 = gain_side if part is None else gain_side * part
                    later[1][x, ch] = start1[x, ch] * inv8 + g1 * (up[1] + down[1] + across[1])
                up, mid = mid, down
        pltpu.make_async_copy(out.at[:, ch], result.at[:, ch], sem.at[c // SUB]).start()

    for c in range(0, chan, SUB):
        ch = slice(c, c + SUB)
        pltpu.make_async_copy(out.at[:, ch], result.at[:, ch], sem.at[c // SUB]).wait()


def relax(inside, merged, above, below, above_side, below_side, left, right, coef):
    count, chan, cells = merged.shape
    held = pltpu.VMEM((count + 2 * WIDTH, chan, cells), F32)
    return pl.pallas_call(
        relax_kernel,
        out_shape=jax.ShapeDtypeStruct(merged.shape, F32),
        in_specs=[whole(pltpu.SMEM)] + [whole()] * 8,
        out_specs=whole(pl.ANY),
        scratch_shapes=[pltpu.VMEM(merged.shape, F32)]
        + [held] * 5
        + [pltpu.SemaphoreType.DMA((chan // SUB,))],
        compiler_params=params(),
        name="relax",
    )(inside, merged, above, below, above_side, below_side, left, right, coef)


def shifted(block, axis, step):
    count = lax.axis_size(axis)
    route = [(i, i + step) for i in range(count) if 0 <= i + step < count]
    return lax.ppermute(block, axis, route)


def local(
    model_state,
    depart_frac,
    depart_cell,
    row_source,
    send_block,
    strip_from,
    strip_into,
    helmholtz_coef,
    vertical_mix,
):
    tile = model_state[0]
    chan = tile.shape[1]
    outgoing = pack_blocks(send_block[0, 0].T, tile)
    arrived = lax.all_to_all(outgoing, ("gx", "gy"), split_axis=0, concat_axis=0, tiled=True)
    coupled = couple(tile, vertical_mix.T)
    slots = arrived.reshape((-1,) + tile.shape[1:])
    arrival, picked = arrive(
        row_source, strip_from[0], slots, coupled, depart_cell[0], depart_frac[0]
    )
    received = lax.ppermute(picked, "panel", [(0, 1), (1, 0)])
    merged, low, high, first, last = merge(strip_into[0], arrival, received)
    right = shifted(low, "gy", -1)
    left = shifted(high, "gy", 1)
    below = shifted(first, "gx", -1)
    above = shifted(last, "gx", 1)
    first_side, last_side = corners(left, right)
    below_side = shifted(first_side, "gx", -1)
    above_side = shifted(last_side, "gx", 1)
    gx, gy = lax.axis_index("gx"), lax.axis_index("gy")
    inside = jnp.stack(
        [gx > 0, gx < lax.axis_size("gx") - 1, gy > 0, gy < lax.axis_size("gy") - 1]
    ).astype(jnp.int32)
    balanced = relax(
        inside,
        merged,
        above,
        below,
        above_side,
        below_side,
        left,
        right,
        helmholtz_coef.reshape(chan, 1),
    )
    return balanced[None]


def solution(mesh):
    in_specs = (
        P("panel", "gx", None, "gy"),
        P("panel", "gx", "gy"),
        P("panel", "gx", "gy"),
        P("panel", ("gx", "gy")),
        P("panel", ("gx", "gy"), None, None),
        P("panel", ("gx", "gy"), None),
        P("panel", ("gx", "gy"), None),
        P(),
        P(),
    )
    out_specs = P("panel", "gx", None, "gy")
    return jax.shard_map(local, mesh=mesh, in_specs=in_specs, out_specs=out_specs, check_vma=False)
```

```python
import functools

import jax
import jax.numpy as jnp
from jax import lax
from jax.experimental import pallas as pl
from jax.experimental.pallas import tpu as pltpu
from jax.sharding import PartitionSpec as P

SWEEPS = 8
WIDTH = 8
PARTS = 4
CHUNK = 16
SUB = 8
F32 = jnp.float32
VMEM_LIMIT = 48 * 1024 * 1024


def whole(space=pltpu.VMEM):
    return pl.BlockSpec(memory_space=space)


def params():
    return pltpu.CompilerParams(vmem_limit_bytes=VMEM_LIMIT)


def cost(flops, moved):
    return pl.CostEstimate(flops=flops, bytes_accessed=moved, transcendentals=0)


def split(place, cells):
    return lax.shift_right_logical(place, cells.bit_length() - 1), place & (cells - 1)


def pack_kernel(listed, tile, out, wanted, sem):
    slots, tiles = wanted.shape
    pltpu.sync_copy(listed, wanted)

    def send(d, sent):
        for k in range(slots):
            block = wanted[k, d]
            filled = block >= 0

            @pl.when(filled)
            def _():
                pltpu.make_async_copy(tile.at[block], out.at[d, k], sem).start()

            sent = sent + jnp.where(filled, 1, 0)
        return sent

    sent = lax.fori_loop(0, tiles, send, 0, unroll=4)

    def wait(_, carry):
        pltpu.make_async_copy(tile.at[0], out.at[0, 0], sem).wait()
        return carry

    lax.fori_loop(0, sent, wait, 0)


def pack_blocks(wanted, tile):
    slots, tiles = wanted.shape
    return pl.pallas_call(
        pack_kernel,
        out_shape=jax.ShapeDtypeStruct((tiles, slots) + tile.shape[1:], F32),
        in_specs=[whole(pltpu.HBM), whole()],
        out_specs=whole(pl.ANY),
        scratch_shapes=[pltpu.SMEM(wanted.shape, jnp.int32), pltpu.SemaphoreType.DMA],
        compiler_params=params(),
        name="pack_blocks",
    )(wanted, tile)


def couple_kernel(tile, mix_t, out):
    mix = mix_t[...] * 0.5

    def row(r, carry):
        out[r] = jnp.dot(mix, tile[r], precision=lax.Precision.HIGHEST, preferred_element_type=F32)
        return carry

    lax.fori_loop(0, tile.shape[0], row, 0, unroll=4)


def couple(tile, mix_t):
    return pl.pallas_call(
        couple_kernel,
        out_shape=jax.ShapeDtypeStruct(tile.shape, F32),
        in_specs=[whole(), whole()],
        out_specs=whole(),
        compiler_params=params(),
        cost_estimate=cost(2 * tile.size * tile.shape[1] * 6, 8 * tile.size),
        name="couple",
    )(tile, mix_t)


def arrive_kernel(rows, strip, slots, coupled, cell, frac, out, picked, fetched, sem):
    count, chan, cells = out.shape

    step = count // PARTS

    def fetch(r, carry, part):
        pltpu.make_async_copy(slots.at[rows[0, r]], fetched.at[r], sem.at[part]).start()
        return carry

    for part in range(PARTS):
        lax.fori_loop(
            part * step, (part + 1) * step, functools.partial(fetch, part=part), 0, unroll=True
        )

    def row(r, carry):
        t = frac[pl.ds(r, 1), :]
        m = jnp.broadcast_to(cell[pl.ds(r, 1), :], (SUB, cells))
        weights = (
            -t * (t - 1.0) * (t - 2.0) / 6.0,
            (t + 1.0) * (t - 1.0) * (t - 2.0) / 2.0,
            -(t + 1.0) * t * (t - 2.0) / 2.0,
            (t + 1.0) * t * (t - 1.0) / 6.0,
        )
        weights = [jnp.broadcast_to(w, (SUB, cells)) for w in weights]
        for c in range(0, chan, SUB):
            block = fetched[r, c : c + SUB, :]
            total = coupled[r, c : c + SUB, :]
            for tap, weight in zip((-1, 0, 1, 2), weights):
                total = total + weight * jnp.take_along_axis(
                    block, m + tap, axis=1, mode="promise_in_bounds"
                )
            out[r, c : c + SUB, :] = total
        return carry

    for part in range(PARTS):
        here = pl.ds(part * step, step)
        pltpu.make_async_copy(slots.at[here], fetched.at[here], sem.at[part]).wait()
        lax.fori_loop(part * step, (part + 1) * step, row, 0, unroll=True)

    lane = lax.broadcasted_iota(jnp.int32, (chan, cells), 1)
    for part in range(picked.shape[1] // cells):

        def pick(j, held):
            place = strip[0, part * cells + j]
            row, at = split(place, cells)
            moved = pltpu.roll(out[row], (j - at) & (cells - 1), 1)
            return jnp.where(lane == j, moved, held)

        held = lax.fori_loop(0, cells, pick, jnp.zeros((chan, cells), F32), unroll=True)
        picked[:, part * cells : (part + 1) * cells] = held


def arrive(rows, strip, slots, coupled, cell, frac):
    return pl.pallas_call(
        arrive_kernel,
        out_shape=(
            jax.ShapeDtypeStruct(coupled.shape, F32),
            jax.ShapeDtypeStruct((coupled.shape[1], strip.shape[1]), F32),
        ),
        in_specs=[whole(pltpu.SMEM), whole(pltpu.SMEM), whole(pl.ANY), whole(), whole(), whole()],
        out_specs=(whole(), whole()),
        scratch_shapes=[pltpu.VMEM(coupled.shape, F32), pltpu.SemaphoreType.DMA((PARTS,))],
        compiler_params=params(),
        name="arrive",
    )(rows, strip, slots, coupled, cell, frac)


def merge_kernel(strip, arrival, received, out, low, high):
    count, chan, cells = out.shape
    out[...] = arrival[...]
    lane = lax.broadcasted_iota(jnp.int32, (chan, cells), 1)
    for part in range(received.shape[1] // cells):

        def put(j, carry):
            place = strip[0, part * cells + j]
            row, at = split(place, cells)
            moved = pltpu.roll(
                received[:, part * cells : (part + 1) * cells], (at - j) & (cells - 1), 1
            )
            pltpu.store(out.at[row], moved, mask=lane == at)
            return carry

        lax.fori_loop(0, cells, put, 0, unroll=32)
    per = cells // WIDTH
    for g in range(count // per):

        def edge(i, held):
            row = out[g * per + i]
            here = (lane // WIDTH) == i
            left = pltpu.roll(row, i * WIDTH, 1)
            right = pltpu.roll(row, (i + 1) * WIDTH & (cells - 1), 1)
            return jnp.where(here, left, held[0]), jnp.where(here, right, held[1])

        empty = jnp.zeros((chan, cells), F32)
        low[g], high[g] = lax.fori_loop(0, per, edge, (empty, empty), unroll=True)


def merge(strip, arrival, received):
    count, chan, cells = arrival.shape
    edge = jax.ShapeDtypeStruct((count * WIDTH // cells, chan, cells), F32)
    return pl.pallas_call(
        merge_kernel,
        out_shape=(jax.ShapeDtypeStruct(arrival.shape, F32), edge, edge),
        in_specs=[whole(pltpu.SMEM), whole(), whole()],
        out_specs=(whole(),) * 3,
        compiler_params=params(),
        name="merge",
    )(strip, arrival, received)


def edge_rows_kernel(merged, left, right, first, last):
    count, chan, cells = merged.shape
    lane = lax.broadcasted_iota(jnp.int32, (chan, cells), 1)
    half = cells // 2
    groups = left.shape[0]
    first[:WIDTH] = merged[:WIDTH]
    first[WIDTH] = jnp.where(lane < half, right[0], pltpu.roll(left[0], half, 1))
    last[:WIDTH] = merged[count - WIDTH :]
    last[WIDTH] = jnp.where(lane < half, pltpu.roll(right[groups - 1], half, 1), left[groups - 1])


def edge_rows(merged, left, right):
    count, chan, cells = merged.shape
    rows = jax.ShapeDtypeStruct((WIDTH + 1, chan, cells), F32)
    return pl.pallas_call(
        edge_rows_kernel,
        out_shape=(rows, rows),
        in_specs=[whole(), whole(), whole()],
        out_specs=(whole(), whole()),
        compiler_params=params(),
        name="edge_rows",
    )(merged, left, right)


def relax_kernel(
    inside,
    merged,
    above,
    below,
    left,
    right,
    coef,
    result,
    out,
    a0,
    a1,
    b0,
    b1,
    start1,
    start0,
    sem,
):
    count, chan, cells = merged.shape
    lane = lax.broadcasted_iota(jnp.int32, (chan, cells), 1)
    is_right = lane < jnp.where(inside[3] > 0, WIDTH, 0)
    is_left = lane >= jnp.where(inside[2] > 0, cells - WIDTH, cells)
    h = coef[...]
    inv = 1.0 / (1.0 + 4.0 * h)
    total = count + 2 * WIDTH
    per = cells // WIDTH
    half = cells // 2

    for at, rows, flag in ((0, above, 0), (WIDTH, below, 1)):
        kept = inside[flag] > 0
        packed = jnp.where(kept, rows[WIDTH], 0.0)
        for i in range(WIDTH):
            start0[at + i] = jnp.where(kept, rows[i], 0.0)
            start1[at // WIDTH * (count + WIDTH) + i] = jnp.where(
                is_right,
                pltpu.roll(packed, (-i * WIDTH) % cells, 1),
                jnp.where(is_left, pltpu.roll(packed, (half - (i + 1) * WIDTH) % cells, 1), 0.0),
            )
    for r in range(count):
        g, i = divmod(r, per)
        start1[WIDTH + r] = jnp.where(
            is_right,
            pltpu.roll(right[g], (-i * WIDTH) % cells, 1),
            jnp.where(is_left, pltpu.roll(left[g], (-(i + 1) * WIDTH) % cells, 1), 0.0),
        )

    lane8 = lax.broadcasted_iota(jnp.int32, (SUB, cells), 1)
    is_first, is_last = lane8 == 0, lane8 == cells - 1
    side = jnp.where(
        lane8 < WIDTH, inside[3], jnp.where(lane8 >= cells - WIDTH, inside[2], 0)
    ).astype(F32)
    lo, hi = inside[0].astype(F32), inside[1].astype(F32)

    def turn(row, beside):
        l0, l1 = pltpu.roll(row, 1, 1), pltpu.roll(beside, 1, 1)
        r0, r1 = pltpu.roll(row, cells - 1, 1), pltpu.roll(beside, cells - 1, 1)
        return (
            jnp.where(is_first, l1, l0) + jnp.where(is_last, r1, r0),
            jnp.where(is_first, l0, l1) + jnp.where(is_last, r0, r1),
        )

    to = lax.broadcasted_iota(jnp.int32, (2 * cells, 2 * cells), 1)
    gap = (to - lax.broadcasted_iota(jnp.int32, (2 * cells, 2 * cells), 0)) & (2 * cells - 1)
    shift = jnp.where((gap == 1) | (gap == 2 * cells - 1), 1.0, 0.0).astype(jnp.bfloat16)

    def first_row(x, ch):
        if x < WIDTH:
            return start0[x, ch]
        return merged[x - WIDTH, ch] if x < WIDTH + count else start0[x - count, ch]

    for c in range(0, chan, SUB):
        ch = slice(c, c + SUB)
        inv8 = jnp.broadcast_to(inv[ch], (SUB, cells))
        gain = jnp.broadcast_to(h[ch] * inv[ch], (SUB, cells))
        gain_side = gain * side

        for s in range(SWEEPS):
            now, later = ((a0, a1), (b0, b1))[:: 1 if s % 2 else -1]
            begin, end = s + 1, total - s - 1

            def held(x):
                if s == 0:
                    return first_row(x, ch), start1[x, ch]
                return now[0][x, ch], now[1][x, ch]

            size = end - begin
            parts = []
            for x0 in range(begin, end, CHUNK):
                x1 = min(x0 + CHUNK, end)
                both = [held(x) for x in range(x0, x1)]
                block = jnp.concatenate(
                    [jnp.concatenate([v[k] for v in both], axis=0) for k in (0, 1)], axis=1
                )
                coarse = block.astype(jnp.bfloat16)
                fine = (block - coarse.astype(F32)).astype(jnp.bfloat16)
                across = jnp.dot(coarse, shift, preferred_element_type=F32) + jnp.dot(
                    fine, shift, preferred_element_type=F32
                )
                for x in range(x0, x1):
                    at = (x - x0) * SUB
                    part = lo if x < WIDTH else hi if x >= WIDTH + count else None
                    g0 = gain if part is None else gain * part
                    up, down = held(x - 1), held(x + 1)
                    new = first_row(x, ch) * inv8 + g0 * (
                        up[0] + down[0] + across[at : at + SUB, :cells]
                    )
                    if s == SWEEPS - 1:
                        out[x - WIDTH, ch] = new
                    else:
                        later[0][x, ch] = new
                        g1 = gain_side if part is None else gain_side * part
                        later[1][x, ch] = start1[x, ch] * inv8 + g1 * (
                            up[1] + down[1] + across[at : at + SUB, cells:]
                        )
        pltpu.make_async_copy(out.at[:, ch], result.at[:, ch], sem.at[c // SUB]).start()

    for c in range(0, chan, SUB):
        ch = slice(c, c + SUB)
        pltpu.make_async_copy(out.at[:, ch], result.at[:, ch], sem.at[c // SUB]).wait()


def relax(inside, merged, above, below, left, right, coef):
    count, chan, cells = merged.shape
    held = pltpu.VMEM((count + 2 * WIDTH, chan, cells), F32)
    return pl.pallas_call(
        relax_kernel,
        out_shape=jax.ShapeDtypeStruct(merged.shape, F32),
        in_specs=[whole(pltpu.SMEM)] + [whole()] * 6,
        out_specs=whole(pl.ANY),
        scratch_shapes=[pltpu.VMEM(merged.shape, F32)]
        + [held] * 5
        + [pltpu.VMEM((2 * WIDTH, chan, cells), F32)]
        + [pltpu.SemaphoreType.DMA((chan // SUB,))],
        compiler_params=params(),
        name="relax",
    )(inside, merged, above, below, left, right, coef)


def shifted(block, axis, step):
    count = lax.axis_size(axis)
    return lax.ppermute(block, axis, [(i, (i + step) % count) for i in range(count)])


def local(
    model_state,
    depart_frac,
    depart_cell,
    row_source,
    send_block,
    strip_from,
    strip_into,
    helmholtz_coef,
    vertical_mix,
):
    tile = model_state[0]
    chan = tile.shape[1]
    outgoing = pack_blocks(send_block[0, 0].T, tile)
    arrived = lax.all_to_all(outgoing, ("gx", "gy"), split_axis=0, concat_axis=0, tiled=True)
    coupled = couple(tile, vertical_mix.T)
    slots = arrived.reshape((-1,) + tile.shape[1:])
    arrival, picked = arrive(
        row_source, strip_from[0], slots, coupled, depart_cell[0], depart_frac[0]
    )
    received = lax.ppermute(picked, "panel", [(0, 1), (1, 0)])
    merged, low, high = merge(strip_into[0], arrival, received)
    right = shifted(low, "gy", -1)
    left = shifted(high, "gy", 1)
    first, last = edge_rows(merged, left, right)
    below = shifted(first, "gx", -1)
    above = shifted(last, "gx", 1)
    gx, gy = lax.axis_index("gx"), lax.axis_index("gy")
    inside = jnp.stack(
        [gx > 0, gx < lax.axis_size("gx") - 1, gy > 0, gy < lax.axis_size("gy") - 1]
    ).astype(jnp.int32)
    balanced = relax(
        inside,
        merged,
        above,
        below,
        left,
        right,
        helmholtz_coef.reshape(chan, 1),
    )
    return balanced[None]


def solution(mesh):
    in_specs = (
        P("panel", "gx", None, "gy"),
        P("panel", "gx", "gy"),
        P("panel", "gx", "gy"),
        P("panel", ("gx", "gy")),
        P("panel", ("gx", "gy"), None, None),
        P("panel", ("gx", "gy"), None),
        P("panel", ("gx", "gy"), None),
        P(),
        P(),
    )
    out_specs = P("panel", "gx", None, "gy")
    return jax.shard_map(local, mesh=mesh, in_specs=in_specs, out_specs=out_specs, check_vma=False)
```

```python
import functools

import jax
import jax.numpy as jnp
from jax import lax
from jax.experimental import pallas as pl
from jax.experimental.pallas import tpu as pltpu
from jax.sharding import PartitionSpec as P

SWEEPS = 8
WIDTH = 8
PARTS = 4
CHUNK = 16
SUB = 8
F32 = jnp.float32
VMEM_LIMIT = 48 * 1024 * 1024


def whole(space=pltpu.VMEM):
    return pl.BlockSpec(memory_space=space)


def params():
    return pltpu.CompilerParams(vmem_limit_bytes=VMEM_LIMIT)


def cost(flops, moved):
    return pl.CostEstimate(flops=flops, bytes_accessed=moved, transcendentals=0)


def terms(value):
    first = value.astype(jnp.bfloat16)
    rest = value - first.astype(F32)
    second = rest.astype(jnp.bfloat16)
    third = (rest - second.astype(F32)).astype(jnp.bfloat16)
    return first, second, third


def ones_where(mask):
    return jnp.where(mask, 1.0, 0.0).astype(jnp.bfloat16)


def pack_kernel(listed, tile, out, wanted, held, sem, list_sem, part_sem):
    slots, tiles = wanted.shape
    step = tile.shape[0] // PARTS
    table = pltpu.make_async_copy(listed, wanted, list_sem)
    table.start()
    parts = []
    for part in range(PARTS):
        here = pl.ds(part * step, step)
        parts.append(pltpu.make_async_copy(tile.at[here], held.at[here], part_sem.at[part]))
        parts[-1].start()
    table.wait()
    for copy in parts:
        copy.wait()

    def send(d, sent):
        for k in range(slots):
            block = wanted[k, d]
            filled = block >= 0

            @pl.when(filled)
            def _():
                pltpu.make_async_copy(held.at[block], out.at[d, k], sem).start()

            sent = sent + jnp.where(filled, 1, 0)
        return sent

    sent = lax.fori_loop(0, tiles, send, 0, unroll=4)

    def wait(_, carry):
        pltpu.make_async_copy(held.at[0], out.at[0, 0], sem).wait()
        return carry

    lax.fori_loop(0, sent, wait, 0)


def pack_blocks(wanted, tile):
    slots, tiles = wanted.shape
    return pl.pallas_call(
        pack_kernel,
        out_shape=jax.ShapeDtypeStruct((tiles, slots) + tile.shape[1:], F32),
        in_specs=[whole(pl.ANY), whole(pl.ANY)],
        out_specs=whole(pl.ANY),
        scratch_shapes=[
            pltpu.SMEM(wanted.shape, jnp.int32),
            pltpu.VMEM(tile.shape, F32),
            pltpu.SemaphoreType.DMA,
            pltpu.SemaphoreType.DMA,
            pltpu.SemaphoreType.DMA((PARTS,)),
        ],
        compiler_params=pltpu.CompilerParams(vmem_limit_bytes=60 * 1024 * 1024),
        name="pack_blocks",
    )(wanted, tile)


def couple_kernel(tile, mix_t, out):
    mix = mix_t[...] * 0.5

    def row(r, carry):
        out[r] = jnp.dot(mix, tile[r], precision=lax.Precision.HIGHEST, preferred_element_type=F32)
        return carry

    lax.fori_loop(0, tile.shape[0], row, 0, unroll=4)


def couple(tile, mix_t):
    return pl.pallas_call(
        couple_kernel,
        out_shape=jax.ShapeDtypeStruct(tile.shape, F32),
        in_specs=[whole(), whole()],
        out_specs=whole(),
        compiler_params=params(),
        cost_estimate=cost(2 * tile.size * tile.shape[1] * 6, 8 * tile.size),
        name="couple",
    )(tile, mix_t)


def arrive_kernel(rows, strip, slots, coupled, cell, frac, out, picked, fetched, offset, sem):
    count, chan, cells = out.shape
    step = count // PARTS

    def fetch(r, carry, part):
        pltpu.make_async_copy(slots.at[rows[0, r]], fetched.at[r], sem.at[part]).start()
        return carry

    for part in range(PARTS):
        lax.fori_loop(
            part * step, (part + 1) * step, functools.partial(fetch, part=part), 0, unroll=True
        )
    offset[...] = strip[...] - lax.broadcasted_iota(jnp.int32, offset.shape, 0)

    def row(r):
        t = frac[r : r + 1, :]
        m = jnp.broadcast_to(cell[r : r + 1, :], (SUB, cells))
        weights = (
            -t * (t - 1.0) * (t - 2.0) / 6.0,
            (t + 1.0) * (t - 1.0) * (t - 2.0) / 2.0,
            -(t + 1.0) * t * (t - 2.0) / 2.0,
            (t + 1.0) * t * (t - 1.0) / 6.0,
        )
        weights = [jnp.broadcast_to(w, (SUB, cells)) for w in weights]
        for c in range(0, chan, SUB):
            block = fetched[r, c : c + SUB, :]
            total = coupled[r, c : c + SUB, :]
            for tap, weight in zip((-1, 0, 1, 2), weights):
                total = total + weight * jnp.take_along_axis(
                    block, m + tap, axis=1, mode="promise_in_bounds"
                )
            out[r, c : c + SUB, :] = total

    total = jnp.zeros((3 * chan, picked.shape[1]), F32)
    for part in range(PARTS):
        here = pl.ds(part * step, step)
        pltpu.make_async_copy(slots.at[here], fetched.at[here], sem.at[part]).wait()
        for r in range(part * step, (part + 1) * step, 2):
            row(r)
            row(r + 1)
            pair = jnp.concatenate([out[r], out[r + 1]], axis=1)
            wanted = ones_where(offset[...] == r * cells)
            total = total + jnp.dot(
                jnp.concatenate(terms(pair), axis=0), wanted, preferred_element_type=F32
            )
    picked[...] = total[:chan] + total[chan : 2 * chan] + total[2 * chan :]


def arrive(rows, strip, slots, coupled, cell, frac):
    return pl.pallas_call(
        arrive_kernel,
        out_shape=(
            jax.ShapeDtypeStruct(coupled.shape, F32),
            jax.ShapeDtypeStruct((coupled.shape[1], strip.shape[1]), F32),
        ),
        in_specs=[whole(pltpu.SMEM), whole(), whole(pl.ANY), whole(), whole(), whole()],
        out_specs=(whole(), whole()),
        scratch_shapes=[
            pltpu.VMEM(coupled.shape, F32),
            pltpu.VMEM((2 * coupled.shape[2], strip.shape[1]), jnp.int32),
            pltpu.SemaphoreType.DMA((PARTS,)),
        ],
        compiler_params=params(),
        name="arrive",
    )(rows, strip, slots, coupled, cell, frac)


def merge_kernel(strip, arrival, received, out, low, high, offset):
    count, chan, cells = out.shape
    offset[...] = strip[...] - lax.broadcasted_iota(jnp.int32, offset.shape, 1)
    size = received.shape[1]
    values = jnp.concatenate(
        [*terms(received[...]), jnp.ones((SUB, size), jnp.bfloat16)], axis=0
    )
    for r in range(0, count, 2):
        placed = jnp.dot(
            values, ones_where(offset[...] == r * cells), preferred_element_type=F32
        )
        value = placed[:chan] + placed[chan : 2 * chan] + placed[2 * chan : 3 * chan]
        hit = jnp.broadcast_to(placed[3 * chan : 3 * chan + 1], value.shape) > 0.5
        for k in range(2):
            at = slice(k * cells, (k + 1) * cells)
            out[r + k] = jnp.where(hit[:, at], value[:, at], arrival[r + k])
    lane = lax.broadcasted_iota(jnp.int32, (chan, cells), 1)
    per = cells // WIDTH
    for g in range(count // per):

        def edge(i, held):
            row = out[g * per + i]
            here = (lane // WIDTH) == i
            left = pltpu.roll(row, i * WIDTH, 1)
            right = pltpu.roll(row, (i + 1) * WIDTH & (cells - 1), 1)
            return jnp.where(here, left, held[0]), jnp.where(here, right, held[1])

        empty = jnp.zeros((chan, cells), F32)
        low[g], high[g] = lax.fori_loop(0, per, edge, (empty, empty), unroll=True)


def merge(strip, arrival, received):
    count, chan, cells = arrival.shape
    edge = jax.ShapeDtypeStruct((count * WIDTH // cells, chan, cells), F32)
    return pl.pallas_call(
        merge_kernel,
        out_shape=(jax.ShapeDtypeStruct(arrival.shape, F32), edge, edge),
        in_specs=[whole(), whole(), whole()],
        out_specs=(whole(),) * 3,
        scratch_shapes=[pltpu.VMEM((strip.shape[0], 2 * cells), jnp.int32)],
        compiler_params=params(),
        name="merge",
    )(strip, arrival, received)


def edge_rows_kernel(merged, left, right, first, last):
    count, chan, cells = merged.shape
    lane = lax.broadcasted_iota(jnp.int32, (chan, cells), 1)
    half = cells // 2
    groups = left.shape[0]
    first[:WIDTH] = merged[:WIDTH]
    first[WIDTH] = jnp.where(lane < half, right[0], pltpu.roll(left[0], half, 1))
    last[:WIDTH] = merged[count - WIDTH :]
    last[WIDTH] = jnp.where(lane < half, pltpu.roll(right[groups - 1], half, 1), left[groups - 1])


def edge_rows(merged, left, right):
    count, chan, cells = merged.shape
    rows = jax.ShapeDtypeStruct((WIDTH + 1, chan, cells), F32)
    return pl.pallas_call(
        edge_rows_kernel,
        out_shape=(rows, rows),
        in_specs=[whole(), whole(), whole()],
        out_specs=(whole(), whole()),
        compiler_params=params(),
        name="edge_rows",
    )(merged, left, right)


def relax_kernel(
    inside,
    merged,
    above,
    below,
    left,
    right,
    coef,
    result,
    out,
    a0,
    a1,
    b0,
    b1,
    start1,
    start0,
    scaled0,
    scaled1,
    sem,
):
    count, chan, cells = merged.shape
    lane = lax.broadcasted_iota(jnp.int32, (chan, cells), 1)
    is_right = lane < jnp.where(inside[3] > 0, WIDTH, 0)
    is_left = lane >= jnp.where(inside[2] > 0, cells - WIDTH, cells)
    h = coef[...]
    inv = 1.0 / (1.0 + 4.0 * h)
    total = count + 2 * WIDTH
    per = cells // WIDTH
    half = cells // 2

    for at, rows, flag in ((0, above, 0), (WIDTH, below, 1)):
        kept = inside[flag] > 0
        packed = jnp.where(kept, rows[WIDTH], 0.0)
        for i in range(WIDTH):
            start0[at + i] = jnp.where(kept, rows[i], 0.0)
            start1[at // WIDTH * (count + WIDTH) + i] = jnp.where(
                is_right,
                pltpu.roll(packed, (-i * WIDTH) % cells, 1),
                jnp.where(is_left, pltpu.roll(packed, (half - (i + 1) * WIDTH) % cells, 1), 0.0),
            )
    for r in range(count):
        g, i = divmod(r, per)
        start1[WIDTH + r] = jnp.where(
            is_right,
            pltpu.roll(right[g], (-i * WIDTH) % cells, 1),
            jnp.where(is_left, pltpu.roll(left[g], (-(i + 1) * WIDTH) % cells, 1), 0.0),
        )

    lane8 = lax.broadcasted_iota(jnp.int32, (SUB, cells), 1)
    side = jnp.where(
        lane8 < WIDTH, inside[3], jnp.where(lane8 >= cells - WIDTH, inside[2], 0)
    ).astype(F32)
    lo, hi = inside[0].astype(F32), inside[1].astype(F32)

    to = lax.broadcasted_iota(jnp.int32, (2 * cells, 2 * cells), 1)
    gap = (to - lax.broadcasted_iota(jnp.int32, (2 * cells, 2 * cells), 0)) & (2 * cells - 1)
    shift = jnp.where((gap == 1) | (gap == 2 * cells - 1), 1.0, 0.0).astype(jnp.bfloat16)

    def first_row(x, ch):
        if x < WIDTH:
            return start0[x, ch]
        return merged[x - WIDTH, ch] if x < WIDTH + count else start0[x - count, ch]

    for c in range(0, chan, SUB):
        ch = slice(c, c + SUB)
        inv8 = jnp.broadcast_to(inv[ch], (SUB, cells))
        gain = jnp.broadcast_to(h[ch] * inv[ch], (SUB, cells))
        gain_side = gain * side

        for x in range(total):
            scaled0[x, ch] = first_row(x, ch) * inv8
            scaled1[x, ch] = start1[x, ch] * inv8

        for s in range(SWEEPS):
            now, later = ((a0, a1), (b0, b1))[:: 1 if s % 2 else -1]
            begin, end = s + 1, total - s - 1

            def held(x):
                if s == 0:
                    return first_row(x, ch), start1[x, ch]
                return now[0][x, ch], now[1][x, ch]

            def store(x, across):
                part = lo if x < WIDTH else hi if x >= WIDTH + count else None
                up, down = held(x - 1), held(x + 1)
                g0 = gain if part is None else gain * part
                new = scaled0[x, ch] + g0 * (up[0] + down[0] + across[0])
                if s == SWEEPS - 1:
                    out[x - WIDTH, ch] = new
                else:
                    later[0][x, ch] = new
                    g1 = gain_side if part is None else gain_side * part
                    later[1][x, ch] = scaled1[x, ch] + g1 * (up[1] + down[1] + across[1])

            x = begin
            while x < end:
                x1 = min(x + CHUNK, end)
                both = [held(y) for y in range(x, x1)]
                block = jnp.concatenate(
                    [jnp.concatenate([v[k] for v in both], axis=0) for k in (0, 1)], axis=1
                )
                coarse = block.astype(jnp.bfloat16)
                fine = (block - coarse.astype(F32)).astype(jnp.bfloat16)
                across = jnp.dot(coarse, shift, preferred_element_type=F32) + jnp.dot(
                    fine, shift, preferred_element_type=F32
                )
                for y in range(x, x1):
                    at = slice((y - x) * SUB, (y - x + 1) * SUB)
                    store(y, (across[at, :cells], across[at, cells:]))
                x = x1
        pltpu.make_async_copy(out.at[:, ch], result.at[:, ch], sem.at[c // SUB]).start()

    for c in range(0, chan, SUB):
        ch = slice(c, c + SUB)
        pltpu.make_async_copy(out.at[:, ch], result.at[:, ch], sem.at[c // SUB]).wait()


def relax(inside, merged, above, below, left, right, coef):
    count, chan, cells = merged.shape
    held = pltpu.VMEM((count + 2 * WIDTH, chan, cells), F32)
    return pl.pallas_call(
        relax_kernel,
        out_shape=jax.ShapeDtypeStruct(merged.shape, F32),
        in_specs=[whole(pltpu.SMEM)] + [whole()] * 6,
        out_specs=whole(pl.ANY),
        scratch_shapes=[pltpu.VMEM(merged.shape, F32)]
        + [held] * 5
        + [pltpu.VMEM((2 * WIDTH, chan, cells), F32)]
        + [held] * 2
        + [pltpu.SemaphoreType.DMA((chan // SUB,))],
        compiler_params=params(),
        name="relax",
    )(inside, merged, above, below, left, right, coef)


def shifted(block, axis, step):
    count = lax.axis_size(axis)
    return lax.ppermute(block, axis, [(i, (i + step) % count) for i in range(count)])


def local(
    model_state,
    depart_frac,
    depart_cell,
    row_source,
    send_block,
    strip_from,
    strip_into,
    helmholtz_coef,
    vertical_mix,
):
    tile = model_state[0]
    chan = tile.shape[1]
    outgoing = pack_blocks(send_block[0, 0].T, tile)
    arrived = lax.all_to_all(outgoing, ("gx", "gy"), split_axis=0, concat_axis=0, tiled=True)
    coupled = couple(tile, vertical_mix.T)
    slots = arrived.reshape((-1,) + tile.shape[1:])
    arrival, picked = arrive(
        row_source, strip_from[0], slots, coupled, depart_cell[0], depart_frac[0]
    )
    received = lax.ppermute(picked, "panel", [(0, 1), (1, 0)])
    merged, low, high = merge(strip_into[0].T, arrival, received)
    right = shifted(low, "gy", -1)
    left = shifted(high, "gy", 1)
    first, last = edge_rows(merged, left, right)
    below = shifted(first, "gx", -1)
    above = shifted(last, "gx", 1)
    gx, gy = lax.axis_index("gx"), lax.axis_index("gy")
    inside = jnp.stack(
        [gx > 0, gx < lax.axis_size("gx") - 1, gy > 0, gy < lax.axis_size("gy") - 1]
    ).astype(jnp.int32)
    balanced = relax(
        inside,
        merged,
        above,
        below,
        left,
        right,
        helmholtz_coef.reshape(chan, 1),
    )
    return balanced[None]


def solution(mesh):
    in_specs = (
        P("panel", "gx", None, "gy"),
        P("panel", "gx", "gy"),
        P("panel", "gx", "gy"),
        P("panel", ("gx", "gy")),
        P("panel", ("gx", "gy"), None, None),
        P("panel", ("gx", "gy"), None),
        P("panel", ("gx", "gy"), None),
        P(),
        P(),
    )
    out_specs = P("panel", "gx", None, "gy")
    return jax.shard_map(local, mesh=mesh, in_specs=in_specs, out_specs=out_specs, check_vma=False)
```

```python
import functools

import jax
import jax.numpy as jnp
from jax import lax
from jax.experimental import pallas as pl
from jax.experimental.pallas import tpu as pltpu
from jax.sharding import PartitionSpec as P

SWEEPS = 8
WIDTH = 8
PARTS = 4
CHUNK = 16
SUB = 8
F32 = jnp.float32
MIB = 1024 * 1024


def whole(space=pltpu.VMEM):
    return pl.BlockSpec(memory_space=space)


def params(mib):
    return pltpu.CompilerParams(vmem_limit_bytes=mib * MIB)


def cost(flops, moved):
    return pl.CostEstimate(flops=flops, bytes_accessed=moved, transcendentals=0)


def terms(value):
    first = value.astype(jnp.bfloat16)
    rest = value - first.astype(F32)
    second = rest.astype(jnp.bfloat16)
    third = (rest - second.astype(F32)).astype(jnp.bfloat16)
    return first, second, third


def ones_where(mask):
    return jnp.where(mask, 1.0, 0.0).astype(jnp.bfloat16)


def pack_kernel(listed, tile, out, wanted, held, sem, list_sem, part_sem):
    slots, tiles = wanted.shape
    step = tile.shape[0] // PARTS
    table = pltpu.make_async_copy(listed, wanted, list_sem)
    table.start()
    parts = []
    for part in range(PARTS):
        here = pl.ds(part * step, step)
        parts.append(pltpu.make_async_copy(tile.at[here], held.at[here], part_sem.at[part]))
        parts[-1].start()
    table.wait()
    for copy in parts:
        copy.wait()

    def send(d, sent):
        for k in range(slots):
            block = wanted[k, d]
            filled = block >= 0

            @pl.when(filled)
            def _():
                pltpu.make_async_copy(held.at[block], out.at[d, k], sem).start()

            sent = sent + jnp.where(filled, 1, 0)
        return sent

    sent = lax.fori_loop(0, tiles, send, 0, unroll=4)

    def wait(_, carry):
        pltpu.make_async_copy(held.at[0], out.at[0, 0], sem).wait()
        return carry

    lax.fori_loop(0, sent, wait, 0)


def pack_blocks(wanted, tile):
    slots, tiles = wanted.shape
    return pl.pallas_call(
        pack_kernel,
        out_shape=jax.ShapeDtypeStruct((tiles, slots) + tile.shape[1:], F32),
        in_specs=[whole(pl.ANY), whole(pl.ANY)],
        out_specs=whole(pl.ANY),
        scratch_shapes=[
            pltpu.SMEM(wanted.shape, jnp.int32),
            pltpu.VMEM(tile.shape, F32),
            pltpu.SemaphoreType.DMA,
            pltpu.SemaphoreType.DMA,
            pltpu.SemaphoreType.DMA((PARTS,)),
        ],
        compiler_params=params(60),
        name="pack_blocks",
    )(wanted, tile)


def prepare_kernel(tile, mix_t, strip, out, columns):
    mix = mix_t[...] * 0.5

    def row(r, carry):
        out[r] = jnp.dot(mix, tile[r], precision=lax.Precision.HIGHEST, preferred_element_type=F32)
        return carry

    lax.fori_loop(0, tile.shape[0], row, 0, unroll=4)
    size, cells = columns.shape
    columns[...] = jnp.broadcast_to(strip[...], (cells, size)).T


def prepare(tile, mix_t, strip):
    return pl.pallas_call(
        prepare_kernel,
        out_shape=(
            jax.ShapeDtypeStruct(tile.shape, F32),
            jax.ShapeDtypeStruct((strip.shape[1], tile.shape[2]), jnp.int32),
        ),
        in_specs=[whole()] * 3,
        out_specs=(whole(), whole()),
        compiler_params=params(16),
        cost_estimate=cost(2 * tile.size * tile.shape[1] * 6, 8 * tile.size),
        name="prepare",
    )(tile, mix_t, strip)


def arrive_kernel(rows, strip, slots, coupled, cell, frac, out, picked, fetched, offset, sem):
    count, chan, cells = out.shape
    step = count // PARTS

    def fetch(r, carry, part):
        pltpu.make_async_copy(slots.at[rows[0, r]], fetched.at[r], sem.at[part]).start()
        return carry

    for part in range(PARTS):
        lax.fori_loop(
            part * step, (part + 1) * step, functools.partial(fetch, part=part), 0, unroll=True
        )
    offset[...] = strip[...] - lax.broadcasted_iota(jnp.int32, offset.shape, 0)

    def row(r):
        t = frac[r : r + 1, :]
        m = jnp.broadcast_to(cell[r : r + 1, :], (SUB, cells))
        weights = (
            -t * (t - 1.0) * (t - 2.0) / 6.0,
            (t + 1.0) * (t - 1.0) * (t - 2.0) / 2.0,
            -(t + 1.0) * t * (t - 2.0) / 2.0,
            (t + 1.0) * t * (t - 1.0) / 6.0,
        )
        weights = [jnp.broadcast_to(w, (SUB, cells)) for w in weights]
        for c in range(0, chan, SUB):
            block = fetched[r, c : c + SUB, :]
            total = coupled[r, c : c + SUB, :]
            for tap, weight in zip((-1, 0, 1, 2), weights):
                total = total + weight * jnp.take_along_axis(
                    block, m + tap, axis=1, mode="promise_in_bounds"
                )
            out[r, c : c + SUB, :] = total

    total = jnp.zeros((3 * chan, picked.shape[1]), F32)
    for part in range(PARTS):
        here = pl.ds(part * step, step)
        pltpu.make_async_copy(slots.at[here], fetched.at[here], sem.at[part]).wait()
        for r in range(part * step, (part + 1) * step, 2):
            row(r)
            row(r + 1)
            pair = jnp.concatenate([out[r], out[r + 1]], axis=1)
            wanted = ones_where(offset[...] == r * cells)
            total = total + jnp.dot(
                jnp.concatenate(terms(pair), axis=0), wanted, preferred_element_type=F32
            )
    picked[...] = total[:chan] + total[chan : 2 * chan] + total[2 * chan :]


def arrive(rows, strip, slots, coupled, cell, frac):
    return pl.pallas_call(
        arrive_kernel,
        out_shape=(
            jax.ShapeDtypeStruct(coupled.shape, F32),
            jax.ShapeDtypeStruct((coupled.shape[1], strip.shape[1]), F32),
        ),
        in_specs=[whole(pltpu.SMEM), whole(), whole(pl.ANY), whole(), whole(), whole()],
        out_specs=(whole(), whole()),
        scratch_shapes=[
            pltpu.VMEM(coupled.shape, F32),
            pltpu.VMEM((2 * coupled.shape[2], strip.shape[1]), jnp.int32),
            pltpu.SemaphoreType.DMA((PARTS,)),
        ],
        compiler_params=params(48),
        name="arrive",
    )(rows, strip, slots, coupled, cell, frac)


def merge_kernel(columns, arrival, received, out, low, high, offset):
    count, chan, cells = out.shape
    for k in range(2):
        at = slice(k * cells, (k + 1) * cells)
        offset[:, at] = (
            columns[...] - lax.broadcasted_iota(jnp.int32, columns.shape, 1) - k * cells
        )
    size = received.shape[1]
    values = jnp.concatenate(
        [*terms(received[...]), jnp.ones((SUB, size), jnp.bfloat16)], axis=0
    )
    for r in range(0, count, 2):
        placed = jnp.dot(
            values, ones_where(offset[...] == r * cells), preferred_element_type=F32
        )
        value = placed[:chan] + placed[chan : 2 * chan] + placed[2 * chan : 3 * chan]
        hit = jnp.broadcast_to(placed[3 * chan : 3 * chan + 1], value.shape) > 0.5
        for k in range(2):
            at = slice(k * cells, (k + 1) * cells)
            out[r + k] = jnp.where(hit[:, at], value[:, at], arrival[r + k])
    lane = lax.broadcasted_iota(jnp.int32, (chan, cells), 1)
    per = cells // WIDTH
    for g in range(count // per):

        def edge(i, held):
            row = out[g * per + i]
            here = (lane // WIDTH) == i
            left = pltpu.roll(row, i * WIDTH, 1)
            right = pltpu.roll(row, (i + 1) * WIDTH & (cells - 1), 1)
            return jnp.where(here, left, held[0]), jnp.where(here, right, held[1])

        empty = jnp.zeros((chan, cells), F32)
        low[g], high[g] = lax.fori_loop(0, per, edge, (empty, empty), unroll=True)


def merge(columns, arrival, received):
    count, chan, cells = arrival.shape
    edge = jax.ShapeDtypeStruct((count * WIDTH // cells, chan, cells), F32)
    return pl.pallas_call(
        merge_kernel,
        out_shape=(jax.ShapeDtypeStruct(arrival.shape, F32), edge, edge),
        in_specs=[whole(), whole(), whole()],
        out_specs=(whole(),) * 3,
        scratch_shapes=[pltpu.VMEM((columns.shape[0], 2 * cells), jnp.int32)],
        compiler_params=params(16),
        name="merge",
    )(columns, arrival, received)


def edge_rows_kernel(merged, left, right, first, last):
    count, chan, cells = merged.shape
    lane = lax.broadcasted_iota(jnp.int32, (chan, cells), 1)
    half = cells // 2
    groups = left.shape[0]
    first[:WIDTH] = merged[:WIDTH]
    first[WIDTH] = jnp.where(lane < half, right[0], pltpu.roll(left[0], half, 1))
    last[:WIDTH] = merged[count - WIDTH :]
    last[WIDTH] = jnp.where(lane < half, pltpu.roll(right[groups - 1], half, 1), left[groups - 1])


def edge_rows(merged, left, right):
    count, chan, cells = merged.shape
    rows = jax.ShapeDtypeStruct((WIDTH + 1, chan, cells), F32)
    return pl.pallas_call(
        edge_rows_kernel,
        out_shape=(rows, rows),
        in_specs=[whole(), whole(), whole()],
        out_specs=(whole(), whole()),
        compiler_params=params(8),
        name="edge_rows",
    )(merged, left, right)


def relax_kernel(
    inside,
    merged,
    above,
    below,
    left,
    right,
    coef,
    result,
    out,
    a0,
    a1,
    b0,
    b1,
    start1,
    start0,
    scaled0,
    scaled1,
    sem,
):
    count, chan, cells = merged.shape
    lane = lax.broadcasted_iota(jnp.int32, (chan, cells), 1)
    is_right = lane < jnp.where(inside[3] > 0, WIDTH, 0)
    is_left = lane >= jnp.where(inside[2] > 0, cells - WIDTH, cells)
    h = coef[...]
    inv = 1.0 / (1.0 + 4.0 * h)
    total = count + 2 * WIDTH
    per = cells // WIDTH
    half = cells // 2

    for at, rows, flag in ((0, above, 0), (WIDTH, below, 1)):
        kept = inside[flag] > 0
        packed = jnp.where(kept, rows[WIDTH], 0.0)
        for i in range(WIDTH):
            start0[at + i] = jnp.where(kept, rows[i], 0.0)
            start1[at // WIDTH * (count + WIDTH) + i] = jnp.where(
                is_right,
                pltpu.roll(packed, (-i * WIDTH) % cells, 1),
                jnp.where(is_left, pltpu.roll(packed, (half - (i + 1) * WIDTH) % cells, 1), 0.0),
            )
    for r in range(count):
        g, i = divmod(r, per)
        start1[WIDTH + r] = jnp.where(
            is_right,
            pltpu.roll(right[g], (-i * WIDTH) % cells, 1),
            jnp.where(is_left, pltpu.roll(left[g], (-(i + 1) * WIDTH) % cells, 1), 0.0),
        )

    lane8 = lax.broadcasted_iota(jnp.int32, (SUB, cells), 1)
    side = jnp.where(
        lane8 < WIDTH, inside[3], jnp.where(lane8 >= cells - WIDTH, inside[2], 0)
    ).astype(F32)
    lo, hi = inside[0].astype(F32), inside[1].astype(F32)

    to = lax.broadcasted_iota(jnp.int32, (2 * cells, 2 * cells), 1)
    gap = (to - lax.broadcasted_iota(jnp.int32, (2 * cells, 2 * cells), 0)) & (2 * cells - 1)
    shift = jnp.where((gap == 1) | (gap == 2 * cells - 1), 1.0, 0.0).astype(jnp.bfloat16)

    def first_row(x, ch):
        if x < WIDTH:
            return start0[x, ch]
        return merged[x - WIDTH, ch] if x < WIDTH + count else start0[x - count, ch]

    for c in range(0, chan, SUB):
        ch = slice(c, c + SUB)
        inv8 = jnp.broadcast_to(inv[ch], (SUB, cells))
        gain = jnp.broadcast_to(h[ch] * inv[ch], (SUB, cells))
        gain_side = gain * side

        for x in range(total):
            scaled0[x, ch] = first_row(x, ch) * inv8
            scaled1[x, ch] = start1[x, ch] * inv8

        for s in range(SWEEPS):
            now, later = ((a0, a1), (b0, b1))[:: 1 if s % 2 else -1]
            begin, end = s + 1, total - s - 1

            def held(x):
                if s == 0:
                    return first_row(x, ch), start1[x, ch]
                return now[0][x, ch], now[1][x, ch]

            def store(x, across):
                part = lo if x < WIDTH else hi if x >= WIDTH + count else None
                up, down = held(x - 1), held(x + 1)
                g0 = gain if part is None else gain * part
                new = scaled0[x, ch] + g0 * (up[0] + down[0] + across[0])
                if s == SWEEPS - 1:
                    out[x - WIDTH, ch] = new
                else:
                    later[0][x, ch] = new
                    g1 = gain_side if part is None else gain_side * part
                    later[1][x, ch] = scaled1[x, ch] + g1 * (up[1] + down[1] + across[1])

            x = begin
            while x < end:
                x1 = min(x + CHUNK, end)
                both = [held(y) for y in range(x, x1)]
                block = jnp.concatenate(
                    [jnp.concatenate([v[k] for v in both], axis=0) for k in (0, 1)], axis=1
                )
                coarse = block.astype(jnp.bfloat16)
                fine = (block - coarse.astype(F32)).astype(jnp.bfloat16)
                across = jnp.dot(coarse, shift, preferred_element_type=F32) + jnp.dot(
                    fine, shift, preferred_element_type=F32
                )
                for y in range(x, x1):
                    at = slice((y - x) * SUB, (y - x + 1) * SUB)
                    store(y, (across[at, :cells], across[at, cells:]))
                x = x1
        pltpu.make_async_copy(out.at[:, ch], result.at[:, ch], sem.at[c // SUB]).start()

    for c in range(0, chan, SUB):
        ch = slice(c, c + SUB)
        pltpu.make_async_copy(out.at[:, ch], result.at[:, ch], sem.at[c // SUB]).wait()


def relax(inside, merged, above, below, left, right, coef):
    count, chan, cells = merged.shape
    held = pltpu.VMEM((count + 2 * WIDTH, chan, cells), F32)
    return pl.pallas_call(
        relax_kernel,
        out_shape=jax.ShapeDtypeStruct(merged.shape, F32),
        in_specs=[whole(pltpu.SMEM)] + [whole()] * 6,
        out_specs=whole(pl.ANY),
        scratch_shapes=[pltpu.VMEM(merged.shape, F32)]
        + [held] * 5
        + [pltpu.VMEM((2 * WIDTH, chan, cells), F32)]
        + [held] * 2
        + [pltpu.SemaphoreType.DMA((chan // SUB,))],
        compiler_params=params(32),
        name="relax",
    )(inside, merged, above, below, left, right, coef)


def shifted(block, axis, step):
    count = lax.axis_size(axis)
    return lax.ppermute(block, axis, [(i, (i + step) % count) for i in range(count)])


def local(
    model_state,
    depart_frac,
    depart_cell,
    row_source,
    send_block,
    strip_from,
    strip_into,
    helmholtz_coef,
    vertical_mix,
):
    tile = model_state[0]
    chan = tile.shape[1]
    outgoing = pack_blocks(send_block[0, 0].T, tile)
    arrived = lax.all_to_all(outgoing, ("gx", "gy"), split_axis=0, concat_axis=0, tiled=True)
    coupled, columns = prepare(tile, vertical_mix.T, strip_into[0])
    slots = arrived.reshape((-1,) + tile.shape[1:])
    arrival, picked = arrive(
        row_source, strip_from[0], slots, coupled, depart_cell[0], depart_frac[0]
    )
    received = lax.ppermute(picked, "panel", [(0, 1), (1, 0)])
    merged, low, high = merge(columns, arrival, received)
    right = shifted(low, "gy", -1)
    left = shifted(high, "gy", 1)
    first, last = edge_rows(merged, left, right)
    below = shifted(first, "gx", -1)
    above = shifted(last, "gx", 1)
    gx, gy = lax.axis_index("gx"), lax.axis_index("gy")
    inside = jnp.stack(
        [gx > 0, gx < lax.axis_size("gx") - 1, gy > 0, gy < lax.axis_size("gy") - 1]
    ).astype(jnp.int32)
    balanced = relax(
        inside,
        merged,
        above,
        below,
        left,
        right,
        helmholtz_coef.reshape(chan, 1),
    )
    return balanced[None]


def solution(mesh):
    in_specs = (
        P("panel", "gx", None, "gy"),
        P("panel", "gx", "gy"),
        P("panel", "gx", "gy"),
        P("panel", ("gx", "gy")),
        P("panel", ("gx", "gy"), None, None),
        P("panel", ("gx", "gy"), None),
        P("panel", ("gx", "gy"), None),
        P(),
        P(),
    )
    out_specs = P("panel", "gx", None, "gy")
    return jax.shard_map(local, mesh=mesh, in_specs=in_specs, out_specs=out_specs, check_vma=False)
```

```python
import functools

import jax
import jax.numpy as jnp
from jax import lax
from jax.experimental import pallas as pl
from jax.experimental.pallas import tpu as pltpu
from jax.sharding import PartitionSpec as P

SWEEPS = 8
WIDTH = 8
PARTS = 4
CHUNK = 16
SUB = 8
F32 = jnp.float32
MIB = 1024 * 1024


def whole(space=pltpu.VMEM):
    return pl.BlockSpec(memory_space=space)


def params(mib):
    return pltpu.CompilerParams(vmem_limit_bytes=mib * MIB)


def cost(flops, moved):
    return pl.CostEstimate(flops=flops, bytes_accessed=moved, transcendentals=0)


def terms(value):
    first = value.astype(jnp.bfloat16)
    rest = value - first.astype(F32)
    second = rest.astype(jnp.bfloat16)
    third = (rest - second.astype(F32)).astype(jnp.bfloat16)
    return first, second, third


def ones_where(mask):
    return jnp.where(mask, 1.0, 0.0).astype(jnp.bfloat16)


def pack_kernel(listed, tile, out, wanted, held, sem, list_sem, part_sem):
    slots, tiles = wanted.shape
    step = tile.shape[0] // PARTS
    table = pltpu.make_async_copy(listed, wanted, list_sem)
    table.start()
    parts = []
    for part in range(PARTS):
        here = pl.ds(part * step, step)
        parts.append(pltpu.make_async_copy(tile.at[here], held.at[here], part_sem.at[part]))
        parts[-1].start()
    table.wait()
    for copy in parts:
        copy.wait()

    def send(d, sent):
        for k in range(slots):
            block = wanted[k, d]
            filled = block >= 0

            @pl.when(filled)
            def _():
                pltpu.make_async_copy(held.at[block], out.at[d, k], sem).start()

            sent = sent + jnp.where(filled, 1, 0)
        return sent

    sent = lax.fori_loop(0, tiles, send, 0, unroll=16)

    def wait(_, carry):
        pltpu.make_async_copy(held.at[0], out.at[0, 0], sem).wait()
        return carry

    lax.fori_loop(0, sent, wait, 0)


def pack_blocks(wanted, tile):
    slots, tiles = wanted.shape
    return pl.pallas_call(
        pack_kernel,
        out_shape=jax.ShapeDtypeStruct((tiles, slots) + tile.shape[1:], F32),
        in_specs=[whole(pl.ANY), whole(pl.ANY)],
        out_specs=whole(pl.ANY),
        scratch_shapes=[
            pltpu.SMEM(wanted.shape, jnp.int32),
            pltpu.VMEM(tile.shape, F32),
            pltpu.SemaphoreType.DMA,
            pltpu.SemaphoreType.DMA,
            pltpu.SemaphoreType.DMA((PARTS,)),
        ],
        compiler_params=params(60),
        name="pack_blocks",
    )(wanted, tile)


def prepare_kernel(tile, mix_t, strip, out, columns):
    mix = mix_t[...] * 0.5

    def row(r, carry):
        out[r] = jnp.dot(mix, tile[r], precision=lax.Precision.HIGHEST, preferred_element_type=F32)
        return carry

    lax.fori_loop(0, tile.shape[0], row, 0, unroll=4)
    size, cells = columns.shape
    columns[...] = jnp.broadcast_to(strip[...], (cells, size)).T


def prepare(tile, mix_t, strip):
    return pl.pallas_call(
        prepare_kernel,
        out_shape=(
            jax.ShapeDtypeStruct(tile.shape, F32),
            jax.ShapeDtypeStruct((strip.shape[1], tile.shape[2]), jnp.int32),
        ),
        in_specs=[whole()] * 3,
        out_specs=(whole(), whole()),
        compiler_params=params(16),
        cost_estimate=cost(2 * tile.size * tile.shape[1] * 6, 8 * tile.size),
        name="prepare",
    )(tile, mix_t, strip)


def arrive_kernel(rows, strip, slots, coupled, cell, frac, out, picked, fetched, offset, sem):
    count, chan, cells = out.shape
    step = count // PARTS

    def fetch(r, carry, part):
        pltpu.make_async_copy(slots.at[rows[0, r]], fetched.at[r], sem.at[part]).start()
        return carry

    for part in range(PARTS):
        lax.fori_loop(
            part * step, (part + 1) * step, functools.partial(fetch, part=part), 0, unroll=True
        )
    offset[...] = strip[...] - lax.broadcasted_iota(jnp.int32, offset.shape, 0)

    def row(r):
        t = frac[r : r + 1, :]
        m = jnp.broadcast_to(cell[r : r + 1, :], (SUB, cells))
        weights = (
            -t * (t - 1.0) * (t - 2.0) / 6.0,
            (t + 1.0) * (t - 1.0) * (t - 2.0) / 2.0,
            -(t + 1.0) * t * (t - 2.0) / 2.0,
            (t + 1.0) * t * (t - 1.0) / 6.0,
        )
        weights = [jnp.broadcast_to(w, (SUB, cells)) for w in weights]
        for c in range(0, chan, SUB):
            block = fetched[r, c : c + SUB, :]
            total = coupled[r, c : c + SUB, :]
            for tap, weight in zip((-1, 0, 1, 2), weights):
                total = total + weight * jnp.take_along_axis(
                    block, m + tap, axis=1, mode="promise_in_bounds"
                )
            out[r, c : c + SUB, :] = total

    total = jnp.zeros((3 * chan, picked.shape[1]), F32)
    for part in range(PARTS):
        here = pl.ds(part * step, step)
        pltpu.make_async_copy(slots.at[here], fetched.at[here], sem.at[part]).wait()
        for r in range(part * step, (part + 1) * step, 2):
            row(r)
            row(r + 1)
            pair = jnp.concatenate([out[r], out[r + 1]], axis=1)
            wanted = ones_where(offset[...] == r * cells)
            total = total + jnp.dot(
                jnp.concatenate(terms(pair), axis=0), wanted, preferred_element_type=F32
            )
    picked[...] = total[:chan] + total[chan : 2 * chan] + total[2 * chan :]


def arrive(rows, strip, slots, coupled, cell, frac):
    return pl.pallas_call(
        arrive_kernel,
        out_shape=(
            jax.ShapeDtypeStruct(coupled.shape, F32),
            jax.ShapeDtypeStruct((coupled.shape[1], strip.shape[1]), F32),
        ),
        in_specs=[whole(pltpu.SMEM), whole(), whole(pl.ANY), whole(), whole(), whole()],
        out_specs=(whole(), whole()),
        scratch_shapes=[
            pltpu.VMEM(coupled.shape, F32),
            pltpu.VMEM((2 * coupled.shape[2], strip.shape[1]), jnp.int32),
            pltpu.SemaphoreType.DMA((PARTS,)),
        ],
        compiler_params=params(48),
        name="arrive",
    )(rows, strip, slots, coupled, cell, frac)


def merge_kernel(columns, arrival, received, out, low, high, offset):
    count, chan, cells = out.shape
    for k in range(2):
        at = slice(k * cells, (k + 1) * cells)
        offset[:, at] = (
            columns[...] - lax.broadcasted_iota(jnp.int32, columns.shape, 1) - k * cells
        )
    size = received.shape[1]
    values = jnp.concatenate(
        [*terms(received[...]), jnp.ones((SUB, size), jnp.bfloat16)], axis=0
    )
    for r in range(0, count, 2):
        placed = jnp.dot(
            values, ones_where(offset[...] == r * cells), preferred_element_type=F32
        )
        value = placed[:chan] + placed[chan : 2 * chan] + placed[2 * chan : 3 * chan]
        hit = jnp.broadcast_to(placed[3 * chan : 3 * chan + 1], value.shape) > 0.5
        for k in range(2):
            at = slice(k * cells, (k + 1) * cells)
            out[r + k] = jnp.where(hit[:, at], value[:, at], arrival[r + k])
    lane = lax.broadcasted_iota(jnp.int32, (chan, cells), 1)
    per = cells // WIDTH
    for g in range(count // per):

        def edge(i, held):
            row = out[g * per + i]
            here = (lane // WIDTH) == i
            left = pltpu.roll(row, i * WIDTH, 1)
            right = pltpu.roll(row, (i + 1) * WIDTH & (cells - 1), 1)
            return jnp.where(here, left, held[0]), jnp.where(here, right, held[1])

        empty = jnp.zeros((chan, cells), F32)
        low[g], high[g] = lax.fori_loop(0, per, edge, (empty, empty), unroll=True)


def merge(columns, arrival, received):
    count, chan, cells = arrival.shape
    edge = jax.ShapeDtypeStruct((count * WIDTH // cells, chan, cells), F32)
    return pl.pallas_call(
        merge_kernel,
        out_shape=(jax.ShapeDtypeStruct(arrival.shape, F32), edge, edge),
        in_specs=[whole(), whole(), whole()],
        out_specs=(whole(),) * 3,
        scratch_shapes=[pltpu.VMEM((columns.shape[0], 2 * cells), jnp.int32)],
        compiler_params=params(16),
        name="merge",
    )(columns, arrival, received)


def edge_rows_kernel(merged, left, right, first, last):
    count, chan, cells = merged.shape
    lane = lax.broadcasted_iota(jnp.int32, (chan, cells), 1)
    half = cells // 2
    groups = left.shape[0]
    first[:WIDTH] = merged[:WIDTH]
    first[WIDTH] = jnp.where(lane < half, right[0], pltpu.roll(left[0], half, 1))
    last[:WIDTH] = merged[count - WIDTH :]
    last[WIDTH] = jnp.where(lane < half, pltpu.roll(right[groups - 1], half, 1), left[groups - 1])


def edge_rows(merged, left, right):
    count, chan, cells = merged.shape
    rows = jax.ShapeDtypeStruct((WIDTH + 1, chan, cells), F32)
    return pl.pallas_call(
        edge_rows_kernel,
        out_shape=(rows, rows),
        in_specs=[whole(), whole(), whole()],
        out_specs=(whole(), whole()),
        compiler_params=params(8),
        name="edge_rows",
    )(merged, left, right)


def unpack_kernel(inside, merged, left, right, coef, beside, ready0, ready1):
    count, chan, cells = merged.shape
    lane = lax.broadcasted_iota(jnp.int32, (chan, cells), 1)
    is_right = lane < jnp.where(inside[3] > 0, WIDTH, 0)
    is_left = lane >= jnp.where(inside[2] > 0, cells - WIDTH, cells)
    inv = jnp.broadcast_to(1.0 / (1.0 + 4.0 * coef[...]), (chan, cells))
    for r in range(count):
        g, i = divmod(r, cells // WIDTH)
        row = jnp.where(
            is_right,
            pltpu.roll(right[g], (-i * WIDTH) % cells, 1),
            jnp.where(is_left, pltpu.roll(left[g], (-(i + 1) * WIDTH) % cells, 1), 0.0),
        )
        beside[r] = row
        ready0[r] = merged[r] * inv
        ready1[r] = row * inv


def unpack(inside, merged, left, right, coef):
    tile = jax.ShapeDtypeStruct(merged.shape, F32)
    return pl.pallas_call(
        unpack_kernel,
        out_shape=(tile,) * 3,
        in_specs=[whole(pltpu.SMEM)] + [whole()] * 4,
        out_specs=(whole(),) * 3,
        compiler_params=params(8),
        cost_estimate=cost(8 * merged.size, 16 * merged.size),
        name="unpack",
    )(inside, merged, left, right, coef)


def relax_kernel(
    inside,
    merged,
    above,
    below,
    beside,
    ready0,
    ready1,
    coef,
    result,
    out,
    a0,
    a1,
    b0,
    b1,
    start1,
    start0,
    scaled0,
    scaled1,
    sem,
):
    count, chan, cells = merged.shape
    lane = lax.broadcasted_iota(jnp.int32, (chan, cells), 1)
    is_right = lane < jnp.where(inside[3] > 0, WIDTH, 0)
    is_left = lane >= jnp.where(inside[2] > 0, cells - WIDTH, cells)
    h = coef[...]
    inv = 1.0 / (1.0 + 4.0 * h)
    total = count + 2 * WIDTH
    half = cells // 2

    for at, rows, flag in ((0, above, 0), (WIDTH, below, 1)):
        kept = inside[flag] > 0
        packed = jnp.where(kept, rows[WIDTH], 0.0)
        for i in range(WIDTH):
            start0[at + i] = jnp.where(kept, rows[i], 0.0)
            start1[at // WIDTH * (count + WIDTH) + i] = jnp.where(
                is_right,
                pltpu.roll(packed, (-i * WIDTH) % cells, 1),
                jnp.where(is_left, pltpu.roll(packed, (half - (i + 1) * WIDTH) % cells, 1), 0.0),
            )

    lane8 = lax.broadcasted_iota(jnp.int32, (SUB, cells), 1)
    side = jnp.where(
        lane8 < WIDTH, inside[3], jnp.where(lane8 >= cells - WIDTH, inside[2], 0)
    ).astype(F32)
    lo, hi = inside[0].astype(F32), inside[1].astype(F32)

    to = lax.broadcasted_iota(jnp.int32, (2 * cells, 2 * cells), 1)
    gap = (to - lax.broadcasted_iota(jnp.int32, (2 * cells, 2 * cells), 0)) & (2 * cells - 1)
    shift = jnp.where((gap == 1) | (gap == 2 * cells - 1), 1.0, 0.0).astype(jnp.bfloat16)

    def side_row(x, ch):
        return beside[x - WIDTH, ch] if WIDTH <= x < WIDTH + count else start1[x, ch]

    def first_row(x, ch):
        if x < WIDTH:
            return start0[x, ch]
        return merged[x - WIDTH, ch] if x < WIDTH + count else start0[x - count, ch]

    for c in range(0, chan, SUB):
        ch = slice(c, c + SUB)
        inv8 = jnp.broadcast_to(inv[ch], (SUB, cells))
        gain = jnp.broadcast_to(h[ch] * inv[ch], (SUB, cells))
        gain_side = gain * side

        for x in (*range(WIDTH), *range(WIDTH + count, total)):
            scaled0[x, ch] = first_row(x, ch) * inv8
            scaled1[x, ch] = start1[x, ch] * inv8

        for s in range(SWEEPS):
            now, later = ((a0, a1), (b0, b1))[:: 1 if s % 2 else -1]
            begin, end = s + 1, total - s - 1

            def held(x):
                if s == 0:
                    return first_row(x, ch), side_row(x, ch)
                return now[0][x, ch], now[1][x, ch]

            def store(x, across):
                part = lo if x < WIDTH else hi if x >= WIDTH + count else None
                up, down = held(x - 1), held(x + 1)
                g0 = gain if part is None else gain * part
                own = WIDTH <= x < WIDTH + count
                new = (ready0[x - WIDTH, ch] if own else scaled0[x, ch]) + g0 * (up[0] + down[0] + across[0])
                if s == SWEEPS - 1:
                    out[x - WIDTH, ch] = new
                else:
                    later[0][x, ch] = new
                    g1 = gain_side if part is None else gain_side * part
                    later[1][x, ch] = (ready1[x - WIDTH, ch] if own else scaled1[x, ch]) + g1 * (up[1] + down[1] + across[1])

            x = begin
            while x < end:
                x1 = min(x + CHUNK, end)
                both = [held(y) for y in range(x, x1)]
                block = jnp.concatenate(
                    [jnp.concatenate([v[k] for v in both], axis=0) for k in (0, 1)], axis=1
                )
                coarse = block.astype(jnp.bfloat16)
                fine = (block - coarse.astype(F32)).astype(jnp.bfloat16)
                ways = shift[:, :cells] if s == SWEEPS - 1 else shift
                across = jnp.dot(coarse, ways, preferred_element_type=F32) + jnp.dot(
                    fine, ways, preferred_element_type=F32
                )
                for y in range(x, x1):
                    at = slice((y - x) * SUB, (y - x + 1) * SUB)
                    store(y, (across[at, :cells], across[at, cells:]))
                x = x1
        pltpu.make_async_copy(out.at[:, ch], result.at[:, ch], sem.at[c // SUB]).start()

    for c in range(0, chan, SUB):
        ch = slice(c, c + SUB)
        pltpu.make_async_copy(out.at[:, ch], result.at[:, ch], sem.at[c // SUB]).wait()


def relax(inside, merged, above, below, beside, ready0, ready1, coef):
    count, chan, cells = merged.shape
    held = pltpu.VMEM((count + 2 * WIDTH, chan, cells), F32)
    return pl.pallas_call(
        relax_kernel,
        out_shape=jax.ShapeDtypeStruct(merged.shape, F32),
        in_specs=[whole(pltpu.SMEM)] + [whole()] * 7,
        out_specs=whole(pl.ANY),
        scratch_shapes=[pltpu.VMEM(merged.shape, F32)]
        + [held] * 5
        + [pltpu.VMEM((2 * WIDTH, chan, cells), F32)]
        + [held] * 2
        + [pltpu.SemaphoreType.DMA((chan // SUB,))],
        compiler_params=params(32),
        name="relax",
    )(inside, merged, above, below, beside, ready0, ready1, coef)


def shifted(block, axis, step):
    count = lax.axis_size(axis)
    return lax.ppermute(block, axis, [(i, (i + step) % count) for i in range(count)])


def local(
    model_state,
    depart_frac,
    depart_cell,
    row_source,
    send_block,
    strip_from,
    strip_into,
    helmholtz_coef,
    vertical_mix,
):
    tile = model_state[0]
    chan = tile.shape[1]
    outgoing = pack_blocks(send_block[0, 0].T, tile)
    arrived = lax.all_to_all(outgoing, ("gx", "gy"), split_axis=0, concat_axis=0, tiled=True)
    coupled, columns = prepare(tile, vertical_mix.T, strip_into[0])
    slots = arrived.reshape((-1,) + tile.shape[1:])
    arrival, picked = arrive(
        row_source, strip_from[0], slots, coupled, depart_cell[0], depart_frac[0]
    )
    received = lax.ppermute(picked, "panel", [(0, 1), (1, 0)])
    merged, low, high = merge(columns, arrival, received)
    right = shifted(low, "gy", -1)
    left = shifted(high, "gy", 1)
    gx, gy = lax.axis_index("gx"), lax.axis_index("gy")
    inside = jnp.stack(
        [gx > 0, gx < lax.axis_size("gx") - 1, gy > 0, gy < lax.axis_size("gy") - 1]
    ).astype(jnp.int32)
    coef = helmholtz_coef.reshape(chan, 1)
    first, last = edge_rows(merged, left, right)
    below = shifted(first, "gx", -1)
    above = shifted(last, "gx", 1)
    beside, ready0, ready1 = unpack(inside, merged, left, right, coef)
    balanced = relax(
        inside,
        merged,
        above,
        below,
        beside,
        ready0,
        ready1,
        coef,
    )
    return balanced[None]


def solution(mesh):
    in_specs = (
        P("panel", "gx", None, "gy"),
        P("panel", "gx", "gy"),
        P("panel", "gx", "gy"),
        P("panel", ("gx", "gy")),
        P("panel", ("gx", "gy"), None, None),
        P("panel", ("gx", "gy"), None),
        P("panel", ("gx", "gy"), None),
        P(),
        P(),
    )
    out_specs = P("panel", "gx", None, "gy")
    return jax.shard_map(local, mesh=mesh, in_specs=in_specs, out_specs=out_specs, check_vma=False)
```
